32 devices in a mesh: group: 2 (over x), tile: 16 (over z, y, core).
Axes of the slice: x: 2, y: 2, z: 4, core: 2. Of those that a mesh axis runs over, the one named last changes fastest.
Arguments:
- tracer: float32 [32, 15, 384, 128], P('group', None, 'tile'), parts along dimension 0, may hold values from 0.01 to 9
- courant_frac: float32 [32, 384, 128], P('group', 'tile'), parts along dimension 0, may hold values from 0.05 to 0.95
- departure_shift: int32 [32, 128], P('group'), parts along dimension 0, may hold values from 0 to 2, as said below
- cell_area: float32 [384, 128], P('tile'), may hold values from 0.6 to 1.6
- adjoint_seed: float32 [32, 15, 384, 128], P('group', None, 'tile'), parts along dimension 0, may hold values from -4 to 6
Outputs:
- tracer_next: float32 [32, 15, 384, 128], P('group', None, 'tile'), parts along dimension 0
- tracer_adjoint: float32 [32, 15, 384, 128], P('group', None, 'tile'), parts along dimension 0
The draws below stay inside these ranges and needn't reach their ends.
There are 2 independent parts, one for each index of `group`. The reference program is written for one: setup_inputs(seed, part) draws one part's arguments, and reference() takes and returns one part's arrays. A program takes and returns all parts, laid end to end along the dimension named above; an argument that names none is the same for every part. Nothing has to cross between parts.
Inputs may be any that keep to these rules, and one draw needn't show every extreme that they name: `departure_shift`: the largest offset is reached in every draw.
All inputs are finite; a program needn't handle non-finite values.
Results may differ from the reference program's by a relative error of at most 0.00002.
Values sent between devices are 32-bit elements; how exact they have to be, the bound alone decides.
No kernel may reach another device: no remote copies, remote signals or barrier semaphores. Data moves between devices by JAX's collectives and lax.ppermute only.
A program may use at most 128 MiB of HBM per device.

```python
import math
import jax
import jax.numpy as jnp
from jax import lax

B = 15
L = 16
NY = 128
MAXOFF = 2
NX = 384


def draw_tracer(key, part):
    key = jax.random.fold_in(key, 1)
    extent = (L, B, NX, NY)
    ramp = 1.0 + 2.0 * lax.broadcasted_iota(jnp.float32, extent, 2) / NX
    logvalues = jax.random.uniform(key, extent, jnp.float32, math.log(0.01), math.log(3.0))
    return jnp.exp(logvalues) * ramp


def draw_departure_shift(key, part):
    key = jax.random.fold_in(key, 2)
    values = jax.random.randint(key, (L, NY), 0, MAXOFF + 1)
    return values.at[0, 0].set(MAXOFF)


def draw_adjoint_seed(key, part):
    key = jax.random.fold_in(key, 3)
    extent = (L, B, NX, NY)
    noise_key, offset_key = jax.random.split(key, 2)
    offsets = jax.random.uniform(offset_key, (L, B, 1, 1), jnp.float32, 0.5, 2.0)
    noise = jnp.clip(jax.random.normal(noise_key, extent, jnp.float32), -4.0, 4.0)
    return jnp.clip(offsets + noise, -4.0, 6.0)


def shard_levels(rng, shape, cuts, least, high):
    def one(dim, blocks):
        heights = jax.random.uniform(jax.random.fold_in(jax.random.fold_in(rng, 6), dim), (blocks,), jnp.float32, least / len(cuts), high / len(cuts))
        return jnp.repeat(jnp.exp(heights), shape[dim] // blocks).reshape((-1,) + (1,) * (len(shape) - dim - 1))

    factor_of = one(*cuts[0])
    for cut in cuts[1:]:
        factor_of = factor_of * one(*cut)
    return factor_of


def setup_inputs(seed: int = 0, part: int = 0) -> dict:
    keys = jax.random.split(jax.random.key(seed), 6)
    part_keys = jax.random.split(jax.random.fold_in(keys[5], part), 6)
    return {
        "tracer": draw_tracer(jax.random.fold_in(jax.random.fold_in(keys[5], part), 71), part),
        "courant_frac": jnp.clip(0.05 + 0.9 * jax.random.uniform(part_keys[1], (L, NX, NY), jnp.float32) ** shard_levels(part_keys[1], (L, NX, NY), ((1, 16),), -0.2, 0.2), 0.05, 0.95),
        "departure_shift": draw_departure_shift(jax.random.fold_in(jax.random.fold_in(keys[5], part), 71), part),
        "cell_area": jnp.clip(0.6 + 1.0 * jax.random.uniform(keys[3], (NX, NY), jnp.float32) ** shard_levels(keys[3], (NX, NY), ((0, 16),), -0.2, 0.2), 0.6, 1.6),
        "adjoint_seed": draw_adjoint_seed(jax.random.fold_in(jax.random.fold_in(keys[5], part), 71), part),
    }


smooth_floor = 0.1

def advect(window, face_frac, shifts, area_cells, first, cell_count):
    face_count = cell_count + 1
    fracs = face_frac[:, first - 1:first - 1 + face_count, :][:, None]
    chosen = shifts[:, None, None, :]

    def take_faces(position):
        return window[:, :, position:position + face_count, :]
    fluxes = jnp.zeros_like(take_faces(first - 1))
    carried = jnp.zeros_like(fluxes)
    for shift_count in range(MAXOFF + 1):
        anchor = first - 1 - shift_count
        minus_two = take_faces(anchor - 2)
        minus_one = take_faces(anchor - 1)
        center = take_faces(anchor)
        plus_one = take_faces(anchor + 1)
        plus_two = take_faces(anchor + 2)
        right_edge = 7.0 / 12.0 * (center + plus_one) - 1.0 / 12.0 * (minus_one + plus_two)
        left_edge = 7.0 / 12.0 * (minus_one + center) - 1.0 / 12.0 * (minus_two + plus_one)
        curvature = 6.0 * center - 3.0 * (left_edge + right_edge)
        partial_flux = fracs * (right_edge - 0.5 * fracs * (right_edge - left_edge - (1.0 - 2.0 * fracs / 3.0) * curvature))
        fluxes = fluxes + jnp.where(chosen == shift_count, carried + partial_flux, 0.0)
        carried = carried + center
    interior = window[:, :, first:first + cell_count, :]
    return interior - (fluxes[:, :, 1:] - fluxes[:, :, :-1]) / area_cells

def forward(tracer, courant_frac, departure_shift, cell_area):
    margin = MAXOFF + 3
    window = jnp.concatenate([tracer[:, :, -margin:], tracer, tracer[:, :, :margin]], axis=2)
    face_frac = jnp.concatenate([courant_frac[:, -margin:], courant_frac, courant_frac[:, :margin]], axis=1)
    advected = advect(window, face_frac, departure_shift, cell_area, margin, NX)
    positive = jnp.sqrt(advected * advected + smooth_floor * smooth_floor)
    mass_before = lax.optimization_barrier(jnp.sum(cell_area * tracer, axis=(2, 3)))
    mass_after = lax.optimization_barrier(jnp.sum(cell_area * positive, axis=(2, 3)))
    return positive * (mass_before / mass_after)[:, :, None, None]

def reference(tracer, courant_frac, departure_shift, cell_area, adjoint_seed):

    def mapping(values):
        return forward(values, courant_frac, departure_shift, cell_area)
    tracer_next, pullback = jax.vjp(mapping, tracer)
    tracer_adjoint, = pullback(adjoint_seed)
    return (tracer_next, tracer_adjoint)
```

```python
import jax
import jax.numpy as jnp
from jax import lax
from jax.experimental import pallas as pl
from jax.experimental.pallas import tpu as pltpu
from jax.sharding import PartitionSpec as P

MAXOFF = 2
FLOOR2 = 0.1 * 0.1
LEFT, RIGHT = 3, 2
OFF = MAXOFF
HALO = LEFT + MAXOFF
T = 8
VMEM_LIMIT = 28 * 2**20
HIGHEST = lax.Precision.HIGHEST


def tap_weights(face, west, inverse, shift_is):
    def taps(f):
        f2 = f * f
        f3 = f2 * f
        alpha = 3.0 * f2 - 2.0 * f3
        beta = f3 - f2
        gamma = f - 2.0 * f2 + f3
        return (
            beta * (-1.0 / 12.0),
            (7.0 / 12.0) * beta - (1.0 / 12.0) * gamma,
            alpha + (7.0 / 12.0) * (beta + gamma),
            (7.0 / 12.0) * gamma - (1.0 / 12.0) * beta,
            gamma * (-1.0 / 12.0),
        )

    east_taps, west_taps = taps(face), taps(west)
    weights = [west_taps[0] * inverse]
    for k in range(4):
        weights.append((west_taps[k + 1] - east_taps[k]) * inverse)
    weights.append(-east_taps[4] * inverse)
    is0, is1, is2 = shift_is
    rest = 1.0 - inverse
    weights[3] = weights[3] + jnp.where(is0, 1.0, inverse)
    weights[4] = weights[4] + jnp.where(is1, rest, 0.0)
    weights[5] = weights[5] + jnp.where(is2, rest, 0.0)
    return weights


def masks(shift_ref, level):
    n = jnp.broadcast_to(shift_ref[pl.ds(level, 1), :], (T, shift_ref.shape[1]))
    return n == 0, n == 1, n == 2


def pick(load, start, shift_is):
    return jnp.where(
        shift_is[0], load(start), jnp.where(shift_is[1], load(start + 1), load(start + 2))
    )


def pick_back(load, start, shift_is):
    return jnp.where(
        shift_is[0], load(start), jnp.where(shift_is[1], load(start - 1), load(start - 2))
    )


def fir(weights, load, start):
    total = weights[0] * load(start)
    for k in range(1, LEFT + RIGHT + 1):
        total = total + weights[k] * load(start + k)
    return total


def floor_parts(advected):
    square = advected * advected + FLOOR2
    root = lax.rsqrt(square)
    return square * root, advected * root


def pack_right_kernel(t_hbm, s_hbm, f_ref, area_ref, out_ref, t_buf, s_buf, sems):
    count, columns, _ = t_hbm.shape
    levels = f_ref.shape[0]
    copies = [
        pltpu.make_async_copy(t_hbm.at[:, pl.ds(columns - T, T), :], t_buf, sems.at[0]),
        pltpu.make_async_copy(s_hbm.at[:, pl.ds(columns - T, T), :], s_buf, sems.at[1]),
    ]
    for copy in copies:
        copy.start()
    width = HALO + MAXOFF
    out_ref[0:T, :] = jnp.zeros((T, out_ref.shape[1]), jnp.float32)
    for copy in copies:
        copy.wait()

    def body(lb, _):
        row = T + lb * width
        out_ref[pl.ds(row + HALO, MAXOFF), :] = s_buf[lb, T - MAXOFF : T, :]
        out_ref[pl.ds(row, HALO), :] = t_buf[lb, T - HALO : T, :]
        return 0

    lax.fori_loop(0, count, body, 0, unroll=8)
    row = T + count * width
    for level in range(levels):
        out_ref[row + LEFT * level : row + LEFT * (level + 1), :] = f_ref[level, columns - LEFT : columns, :]
    row = row + LEFT * levels
    out_ref[row : row + MAXOFF, :] = area_ref[columns - MAXOFF : columns, :]
    end = out_ref.shape[0]
    out_ref[row + MAXOFF : end, :] = jnp.zeros((end - row - MAXOFF, out_ref.shape[1]), jnp.float32)


def interior_kernel(
    t_hbm, s_hbm, f_ref, area_ref, n_ref,
    tv_ref, sv_ref, adv_ref, w_ref, ap_ref, red_ref, out_ref,
    part, sems,
):
    count, columns, rows = t_hbm.shape
    levels = f_ref.shape[0]
    bins = count // levels
    chunks = 4
    per = levels // chunks
    copies = []
    for c in range(chunks):
        span = pl.ds(c * per * bins, per * bins)
        copies.append(
            (
                pltpu.make_async_copy(t_hbm.at[span], tv_ref.at[span, pl.ds(T, columns), :], sems.at[0, c]),
                pltpu.make_async_copy(s_hbm.at[span], sv_ref.at[span, pl.ds(T, columns), :], sems.at[1, c]),
            )
        )
        copies[c][0].start()
        copies[c][1].start()

    tiles = range(1, columns // T)
    width = 2 * HALO

    def level_body(level, _):
        shift_is = masks(n_ref, level)
        weights, areas = [], []
        for v in tiles:
            cell = T * v - OFF
            face = pick(lambda r: f_ref[level, pl.ds(r, T), :], cell, shift_is)
            west = pick(lambda r: f_ref[level, pl.ds(r, T), :], cell - 1, shift_is)
            area = pick(lambda r: area_ref[pl.ds(r, T), :], cell, shift_is)
            w = tap_weights(face, west, 1.0 / area, shift_is)
            for k, value in enumerate(w):
                w_ref[level, k, pl.ds(T * v, T), :] = value
            ap_ref[level, pl.ds(T * v, T), :] = area
            weights.append(w)
            areas.append(area)

        def bin_body(b, _):
            lb = level * bins + b
            mass = area_ref[0:T, :] * tv_ref[lb, T : 2 * T, :]
            for v in range(1, columns // T):
                mass = mass + area_ref[T * v : T * v + T, :] * tv_ref[lb, T * v + T : T * v + 2 * T, :]
            after = dot = None
            for v, w, area in zip(tiles, weights, areas):
                cell = T * v - OFF
                advected = fir(w, lambda r: tv_ref[lb, pl.ds(T + r, T), :], cell - LEFT)
                adv_ref[lb, pl.ds(T * v, T), :] = advected
                positive, _ = floor_parts(advected)
                seed = pick(lambda r: sv_ref[lb, pl.ds(T + r, T), :], cell, shift_is)
                after = area * positive if after is None else after + area * positive
                dot = seed * positive if dot is None else dot + seed * positive
            for k, value in enumerate((mass, after, dot)):
                part[k, pl.ds(lb * T, T), :] = value
            row = T + lb * width
            out_ref[pl.ds(row, HALO), :] = tv_ref[lb, T : T + HALO, :]
            out_ref[pl.ds(row + HALO, HALO), :] = sv_ref[lb, T : T + HALO, :]
            return 0

        lax.fori_loop(0, bins, bin_body, 0, unroll=3)
        return 0

    for c in range(chunks):
        copies[c][0].wait()
        copies[c][1].wait()
        lax.fori_loop(c * per, (c + 1) * per, level_body, 0)

    out_ref[0:T, :] = jnp.zeros((T, rows), jnp.float32)
    row = T + count * width
    for level in range(levels):
        out_ref[row + HALO * level : row + HALO * (level + 1), :] = f_ref[level, 0:HALO, :]
    row = row + HALO * levels
    out_ref[row : row + HALO, :] = area_ref[0:HALO, :]
    end = out_ref.shape[0]
    out_ref[row + HALO : end, :] = jnp.zeros((end - row - HALO, rows), jnp.float32)

    reduce_rows(part, red_ref, 3, count)


def reduce_rows(part, red_ref, kinds, count):
    def body(g, _):
        for k in range(kinds):
            total = part[k, pl.ds(g * T * T, T, stride=T), :]
            for s in range(1, T):
                total = total + part[k, pl.ds(g * T * T + s, T, stride=T), :]
            red_ref[k, pl.ds(g * T, T), :] = total
        return 0

    lax.fori_loop(0, count // T, body, 0, unroll=2)


def left_kernel(
    m_ref, tv_in, sv_in, adv_in, w_in, ap_in, red_ref, f_ref, area_ref, n_ref,
    tv_ref, sv_ref, adv_ref, w_ref, ap_ref, sum_ref,
    part, red_new, f_buf, area_buf,
):
    count = tv_ref.shape[0]
    levels = f_ref.shape[0]
    bins = count // levels
    rows = f_ref.shape[2]
    width = HALO + MAXOFF
    f_row = T + count * width
    area_row = f_row + LEFT * levels
    area_buf[0:T, :] = m_ref[area_row - (T - MAXOFF) : area_row + MAXOFF, :]
    area_buf[T : 2 * T, :] = area_ref[0:T, :]
    cell = -OFF

    def level_body(level, _):
        shift_is = masks(n_ref, level)
        f_buf[level, 0:T, :] = m_ref[pl.ds(f_row + LEFT * level - (T - LEFT), T), :]
        f_buf[level, T : 2 * T, :] = f_ref[level, 0:T, :]
        face = pick(lambda r: f_buf[level, pl.ds(T + r, T), :], cell, shift_is)
        west = pick(lambda r: f_buf[level, pl.ds(T + r, T), :], cell - 1, shift_is)
        area = pick(lambda r: area_buf[pl.ds(T + r, T), :], cell, shift_is)
        w = tap_weights(face, west, 1.0 / area, shift_is)
        for k, value in enumerate(w):
            w_ref[level, k, 0:T, :] = value
        ap_ref[level, 0:T, :] = area

        def fill_body(b, _):
            lb = level * bins + b
            row = T + lb * width
            tv_ref[lb, 0:T, :] = m_ref[pl.ds(row - (T - HALO), T), :]
            sv_ref[lb, 0:T, :] = m_ref[pl.ds(row + HALO - (T - MAXOFF), T), :]
            return 0

        lax.fori_loop(0, bins, fill_body, 0, unroll=True)

        def bin_body(b, _):
            lb = level * bins + b
            advected = fir(w, lambda r: tv_ref[lb, pl.ds(T + r, T), :], cell - LEFT)
            adv_ref[lb, 0:T, :] = advected
            positive, _ = floor_parts(advected)
            seed = pick(lambda r: sv_ref[lb, pl.ds(T + r, T), :], cell, shift_is)
            part[0, pl.ds(lb * T, T), :] = area * positive
            part[1, pl.ds(lb * T, T), :] = seed * positive
            return 0

        lax.fori_loop(0, bins, bin_body, 0, unroll=5)
        return 0

    lax.fori_loop(0, levels, level_body, 0)
    reduce_rows(part, red_new, 2, count)
    ones = jnp.ones((T, rows), jnp.float32)
    for k in range(3):
        values = red_ref[k] if k == 0 else red_ref[k] + red_new[k - 1]
        total = lax.dot_general(
            ones, values, (((1,), (1,)), ((), ())), precision=HIGHEST, preferred_element_type=jnp.float32
        )
        for peer in range(sum_ref.shape[0]):
            sum_ref[peer, k : k + 1, :] = total[0:1, :]


def main_kernel(
    g_ref, sv_ref, adv_ref, w_ref, ap_ref, area_ref, n_ref,
    next_hbm, adj_hbm, scale_ref,
    s_buf, next_buf, adj_buf, sems,
):
    count, rows = scale_ref.shape[1:]
    levels = n_ref.shape[0]
    bins = count // levels
    peers = g_ref.shape[0]
    tiles = next_buf.shape[1] // T
    ones = jnp.ones((peers, rows), jnp.float32)
    sums = [
        lax.dot_general(
            g_ref[:, k, :], ones, (((0,), (0,)), ((), ())), precision=HIGHEST, preferred_element_type=jnp.float32
        )
        for k in range(3)
    ]
    mass_before, mass_after, seed_dot = sums
    direct = seed_dot / mass_after
    rescale = mass_before / mass_after
    scale_ref[0] = rescale
    scale_ref[1] = rescale * direct
    scale_ref[2] = direct

    def copies(level):
        span = pl.ds(level * bins, bins)
        return (
            pltpu.make_async_copy(next_buf.at[span], next_hbm.at[span, pl.ds(0, tiles * T), :], sems.at[0, level]),
            pltpu.make_async_copy(adj_buf.at[span], adj_hbm.at[span, pl.ds(0, tiles * T), :], sems.at[1, level]),
        )

    def level_body(level, _):
        shift_is = masks(n_ref, level)
        areas = [ap_ref[level, T * v : T * v + T, :] for v in range(tiles + 1)]

        def seed_body(b, _):
            lb = level * bins + b
            rescale = scale_ref[0, pl.ds(lb, 1), :]
            feedback = scale_ref[1, pl.ds(lb, 1), :]
            for v in range(tiles + 1):
                _, ratio = floor_parts(adv_ref[lb, T * v : T * v + T, :])
                seed = pick(lambda r: sv_ref[lb, pl.ds(T + r, T), :], T * v - OFF, shift_is)
                s_buf[b, T * v : T * v + T, :] = (rescale * seed - feedback * areas[v]) * ratio
            return 0

        lax.fori_loop(0, bins, seed_body, 0, unroll=3)
        weights = [
            [w_ref[level, k, pl.ds(T * q + OFF + LEFT - k, T), :] for k in range(LEFT + RIGHT + 1)]
            for q in range(tiles)
        ]

        def bin_body(b, _):
            lb = level * bins + b
            rescale = scale_ref[0, pl.ds(lb, 1), :]
            direct = scale_ref[2, pl.ds(lb, 1), :]
            for q in range(tiles):
                total = area_ref[T * q : T * q + T, :] * direct
                for k in range(LEFT + RIGHT + 1):
                    total = total + weights[q][k] * s_buf[b, pl.ds(T * q + OFF + LEFT - k, T), :]
                adj_buf[lb, T * q : T * q + T, :] = total
                advected = pick_back(lambda r: adv_ref[lb, pl.ds(r, T), :], T * q + OFF, shift_is)
                positive, _ = floor_parts(advected)
                next_buf[lb, T * q : T * q + T, :] = positive * rescale
            return 0

        lax.fori_loop(0, bins, bin_body, 0, unroll=3)
        for copy in copies(level):
            copy.start()
        return 0

    lax.fori_loop(0, levels, level_body, 0)

    def wait_body(level, _):
        for copy in copies(level):
            copy.wait()
        return 0

    lax.fori_loop(0, levels, wait_body, 0)


def right_kernel(
    m_ref, tv_ref, sv_ref, adv_ref, w_ref, ap_ref, scale_ref, f_ref, area_ref, n_ref, next_in, adj_in,
    next_hbm, adj_hbm,
    t_buf, seed_buf, adv_buf, w_buf, f_buf, area_buf, s_buf, next_buf, adj_buf, sems,
):
    count = tv_ref.shape[0]
    levels, columns, rows = f_ref.shape
    bins = count // levels
    width = 2 * HALO
    f_row = T + count * width
    area_row = f_row + HALO * levels
    last = columns - T
    area_buf[0:T, :] = area_ref[last:columns, :]
    area_buf[T : 2 * T, :] = m_ref[area_row : area_row + T, :]
    cell = T - OFF

    def copies(level):
        span = pl.ds(level * bins, bins)
        return (
            pltpu.make_async_copy(next_buf.at[span], next_hbm.at[span, pl.ds(last, T), :], sems.at[0, level]),
            pltpu.make_async_copy(adj_buf.at[span], adj_hbm.at[span, pl.ds(last, T), :], sems.at[1, level]),
        )

    def level_body(level, _):
        shift_is = masks(n_ref, level)
        f_buf[level, 0:T, :] = f_ref[level, last:columns, :]
        f_buf[level, T : 2 * T, :] = m_ref[pl.ds(f_row + HALO * level, T), :]
        face = pick(lambda r: f_buf[level, pl.ds(r, T), :], cell, shift_is)
        west = pick(lambda r: f_buf[level, pl.ds(r, T), :], cell - 1, shift_is)
        area = pick(lambda r: area_buf[pl.ds(r, T), :], cell, shift_is)
        w = tap_weights(face, west, 1.0 / area, shift_is)
        for k, value in enumerate(w):
            w_buf[level, k, 0:T, :] = w_ref[level, k, last : last + T, :]
            w_buf[level, k, T : 2 * T, :] = value
        areas = [ap_ref[level, last : last + T, :], area]

        def fill_body(b, _):
            lb = level * bins + b
            row = T + lb * width
            t_buf[b, 0:T, :] = tv_ref[lb, columns : columns + T, :]
            t_buf[b, T : 2 * T, :] = m_ref[pl.ds(row, T), :]
            seed_buf[b, 0:T, :] = sv_ref[lb, columns : columns + T, :]
            seed_buf[b, T : 2 * T, :] = m_ref[pl.ds(row + HALO, T), :]
            adv_buf[b, 0:T, :] = adv_ref[lb, last : last + T, :]
            return 0

        lax.fori_loop(0, bins, fill_body, 0, unroll=True)

        def seed_body(b, _):
            lb = level * bins + b
            rescale = scale_ref[0, pl.ds(lb, 1), :]
            feedback = scale_ref[1, pl.ds(lb, 1), :]
            advected = fir(w, lambda r: t_buf[b, pl.ds(r, T), :], cell - LEFT)
            adv_buf[b, T : 2 * T, :] = advected
            for v, value in enumerate((adv_buf[b, 0:T, :], advected)):
                _, ratio = floor_parts(value)
                if v == 0:
                    seed = pick(lambda r: sv_ref[lb, pl.ds(T + last + r, T), :], -OFF, shift_is)
                else:
                    seed = pick(lambda r: seed_buf[b, pl.ds(r, T), :], cell, shift_is)
                s_buf[b, T * v : T * v + T, :] = (rescale * seed - feedback * areas[v]) * ratio
            return 0

        lax.fori_loop(0, bins, seed_body, 0, unroll=3)
        weights = [w_buf[level, k, pl.ds(OFF + LEFT - k, T), :] for k in range(LEFT + RIGHT + 1)]

        def bin_body(b, _):
            lb = level * bins + b
            rescale = scale_ref[0, pl.ds(lb, 1), :]
            total = area_buf[0:T, :] * scale_ref[2, pl.ds(lb, 1), :]
            for k in range(LEFT + RIGHT + 1):
                total = total + weights[k] * s_buf[b, pl.ds(OFF + LEFT - k, T), :]
            adj_buf[lb] = total
            advected = pick_back(lambda r: adv_buf[b, pl.ds(r, T), :], OFF, shift_is)
            positive, _ = floor_parts(advected)
            next_buf[lb] = positive * rescale
            return 0

        lax.fori_loop(0, bins, bin_body, 0, unroll=3)
        for copy in copies(level):
            copy.start()
        return 0

    lax.fori_loop(0, levels, level_body, 0)

    def wait_body(level, _):
        for copy in copies(level):
            copy.wait()
        return 0

    lax.fori_loop(0, levels, wait_body, 0)


def padded(rows):
    return (rows + 2 * T - 1) // T * T


def shards(tracer, courant_frac, departure_shift, cell_area, adjoint_seed):
    levels, bins, columns, rows = tracer.shape
    count = levels * bins
    f32 = jnp.float32
    tile = lax.axis_size("tile")
    to_right = [(i, (i + 1) % tile) for i in range(tile)]
    to_left = [(target, source) for source, target in to_right]
    t = tracer.reshape(count, columns, rows)
    seed = adjoint_seed.reshape(count, columns, rows)
    hbm = pl.BlockSpec(memory_space=pl.ANY)
    vmem = pl.BlockSpec(memory_space=pltpu.VMEM)
    params = pltpu.CompilerParams(vmem_limit_bytes=VMEM_LIMIT)
    dma = pltpu.SemaphoreType.DMA

    def held(x):
        return pltpu.with_memory_space_constraint(x, pltpu.VMEM)

    def cost(flops, nbytes):
        return pl.CostEstimate(flops=flops, bytes_accessed=nbytes, transcendentals=0)

    right_rows = padded(T + count * (HALO + MAXOFF) + LEFT * levels + MAXOFF)
    left_rows = padded(T + 2 * count * HALO + HALO * levels + HALO)
    size = 4 * count * columns * rows

    message_right = pl.pallas_call(
        pack_right_kernel,
        out_shape=jax.ShapeDtypeStruct((right_rows, rows), f32),
        in_specs=[hbm, hbm, vmem, vmem],
        out_specs=vmem,
        scratch_shapes=[pltpu.VMEM((count, T, rows), f32), pltpu.VMEM((count, T, rows), f32), dma((2,))],
        compiler_params=params,
        cost_estimate=cost(0, size),
        name="pack_right",
    )(t, seed, courant_frac, cell_area)
    from_left = lax.ppermute(message_right, "tile", to_right)

    tv, sv, adv, w, ap, red, message_left = pl.pallas_call(
        interior_kernel,
        out_shape=(
            pltpu.VMEM((count, columns + 2 * T, rows), f32),
            pltpu.VMEM((count, columns + 2 * T, rows), f32),
            pltpu.VMEM((count, columns, rows), f32),
            pltpu.VMEM((levels, LEFT + RIGHT + 1, columns, rows), f32),
            pltpu.VMEM((levels, columns, rows), f32),
            pltpu.VMEM((3, count, rows), f32),
            jax.ShapeDtypeStruct((left_rows, rows), f32),
        ),
        in_specs=[hbm, hbm, vmem, vmem, vmem],
        out_specs=(vmem,) * 7,
        scratch_shapes=[pltpu.VMEM((3, count * T, rows), f32), dma((2, 4))],
        compiler_params=params,
        cost_estimate=cost(30 * size, 4 * size),
        name="interior",
    )(t, seed, courant_frac, cell_area, departure_shift)

    from_left, message_left = lax.optimization_barrier((from_left, message_left))
    from_right = lax.ppermute(message_left, "tile", to_left)

    tv, sv, adv, w, ap, sums = pl.pallas_call(
        left_kernel,
        out_shape=(
            pltpu.VMEM(tv.shape, f32),
            pltpu.VMEM(sv.shape, f32),
            pltpu.VMEM(adv.shape, f32),
            pltpu.VMEM(w.shape, f32),
            pltpu.VMEM(ap.shape, f32),
            jax.ShapeDtypeStruct((tile, 3, count), f32),
        ),
        in_specs=[vmem] * 10,
        out_specs=(vmem,) * 6,
        input_output_aliases={1: 0, 2: 1, 3: 2, 4: 3, 5: 4},
        scratch_shapes=[
            pltpu.VMEM((2, count * T, rows), f32),
            pltpu.VMEM((2, count, rows), f32),
            pltpu.VMEM((levels, 2 * T, rows), f32),
            pltpu.VMEM((2 * T, rows), f32),
        ],
        compiler_params=params,
        cost_estimate=cost(10 * size, size),
        name="left_edge",
    )(from_left, held(tv), held(sv), held(adv), held(w), held(ap), held(red), courant_frac, cell_area, departure_shift)

    sums = lax.all_to_all(sums, "tile", 0, 0)

    main = columns - T
    tracer_next, tracer_adjoint, scale = pl.pallas_call(
        main_kernel,
        out_shape=(
            jax.ShapeDtypeStruct((count, columns, rows), f32),
            jax.ShapeDtypeStruct((count, columns, rows), f32),
            pltpu.VMEM((3, count, rows), f32),
        ),
        in_specs=[vmem] * 7,
        out_specs=(hbm, hbm, vmem),
        scratch_shapes=[
            pltpu.VMEM((bins, columns, rows), f32),
            pltpu.VMEM((count, main, rows), f32),
            pltpu.VMEM((count, main, rows), f32),
            dma((2, levels)),
        ],
        compiler_params=params,
        cost_estimate=cost(30 * size, 4 * size),
        name="main_part",
    )(sums, held(sv), held(adv), held(w), held(ap), cell_area, departure_shift)

    tracer_next, tracer_adjoint = pl.pallas_call(
        right_kernel,
        out_shape=(
            jax.ShapeDtypeStruct((count, columns, rows), f32),
            jax.ShapeDtypeStruct((count, columns, rows), f32),
        ),
        in_specs=[vmem] * 10 + [hbm, hbm],
        out_specs=(hbm, hbm),
        input_output_aliases={10: 0, 11: 1},
        scratch_shapes=[
            pltpu.VMEM((bins, 2 * T, rows), f32),
            pltpu.VMEM((bins, 2 * T, rows), f32),
            pltpu.VMEM((bins, 2 * T, rows), f32),
            pltpu.VMEM((levels, LEFT + RIGHT + 1, 2 * T, rows), f32),
            pltpu.VMEM((levels, 2 * T, rows), f32),
            pltpu.VMEM((2 * T, rows), f32),
            pltpu.VMEM((bins, 2 * T, rows), f32),
            pltpu.VMEM((count, T, rows), f32),
            pltpu.VMEM((count, T, rows), f32),
            dma((2, levels)),
        ],
        compiler_params=params,
        cost_estimate=cost(10 * size, size),
        name="right_edge",
    )(
        from_right, held(tv), held(sv), held(adv), held(w), held(ap), held(scale),
        courant_frac, cell_area, departure_shift, tracer_next, tracer_adjoint,
    )
    return tracer_next.reshape(tracer.shape), tracer_adjoint.reshape(tracer.shape)


def solution(mesh):
    return jax.shard_map(
        shards,
        mesh=mesh,
        in_specs=(
            P("group", None, "tile", None),
            P("group", "tile", None),
            P("group", None),
            P("tile", None),
            P("group", None, "tile", None),
        ),
        out_specs=(P("group", None, "tile", None), P("group", None, "tile", None)),
        check_vma=False,
    )
```

```python
import jax
import jax.numpy as jnp
from jax import lax
from jax.experimental import pallas as pl
from jax.experimental.pallas import tpu as pltpu
from jax.sharding import PartitionSpec as P

MAXOFF = 2
FLOOR2 = 0.1 * 0.1
LEFT, RIGHT = 3, 2
OFF = MAXOFF
HALO = LEFT + MAXOFF
T = 8
VMEM_LIMIT = 20 * 2**20
MAIN_FLOPS = 3000
HIGHEST = lax.Precision.HIGHEST


def tap_weights(face, west, inverse, shift_is):
    def taps(f):
        f2 = f * f
        f3 = f2 * f
        alpha = 3.0 * f2 - 2.0 * f3
        beta = f3 - f2
        gamma = f - 2.0 * f2 + f3
        return (
            beta * (-1.0 / 12.0),
            (7.0 / 12.0) * beta - (1.0 / 12.0) * gamma,
            alpha + (7.0 / 12.0) * (beta + gamma),
            (7.0 / 12.0) * gamma - (1.0 / 12.0) * beta,
            gamma * (-1.0 / 12.0),
        )

    east_taps, west_taps = taps(face), taps(west)
    weights = [west_taps[0] * inverse]
    for k in range(4):
        weights.append((west_taps[k + 1] - east_taps[k]) * inverse)
    weights.append(-east_taps[4] * inverse)
    is0, is1, is2 = shift_is
    rest = 1.0 - inverse
    weights[3] = weights[3] + jnp.where(is0, 1.0, inverse)
    weights[4] = weights[4] + jnp.where(is1, rest, 0.0)
    weights[5] = weights[5] + jnp.where(is2, rest, 0.0)
    return weights


def masks(shift_ref, level):
    n = jnp.broadcast_to(shift_ref[pl.ds(level, 1), :], (T, shift_ref.shape[1]))
    return n == 0, n == 1, n == 2


def pick(load, start, shift_is):
    return jnp.where(
        shift_is[0], load(start), jnp.where(shift_is[1], load(start + 1), load(start + 2))
    )


def pick_back(load, start, shift_is):
    return jnp.where(
        shift_is[0], load(start), jnp.where(shift_is[1], load(start - 1), load(start - 2))
    )


def pick_first(load, shift_is):
    first = load(0)
    two_down = jnp.concatenate([first[T - 2 : T], first[0 : T - 2]], axis=0)
    one_down = jnp.concatenate([first[T - 1 : T], first[0 : T - 1]], axis=0)
    return jnp.where(shift_is[0], two_down, jnp.where(shift_is[1], one_down, first))


def in_chunks(levels, count):
    edges = [levels * c // count for c in range(count + 1)]
    return list(zip(edges[:-1], edges[1:]))


def fir(weights, load, start):
    total = weights[0] * load(start)
    for k in range(1, LEFT + RIGHT + 1):
        total = total + weights[k] * load(start + k)
    return total


def floor_parts(advected):
    square = advected * advected + FLOOR2
    root = lax.rsqrt(square)
    return square * root, advected * root


def pack_right_kernel(t_hbm, s_hbm, f_hbm, area_hbm, n_hbm, out_ref, t_buf, s_buf, f_buf, area_buf, n_buf, sems, small):
    count, columns, rows = t_hbm.shape
    levels = f_hbm.shape[0]
    bins = count // levels
    chunks = sems.shape[1]
    per = levels // chunks
    tail = pl.ds(columns - T, T)
    others = [
        pltpu.make_async_copy(n_hbm, n_buf, small.at[0]),
        pltpu.make_async_copy(f_hbm.at[:, tail, :], f_buf, small.at[1]),
        pltpu.make_async_copy(area_hbm.at[tail, :], area_buf, small.at[2]),
    ]
    others[0].start()
    copies = []
    for c in range(chunks):
        span = pl.ds(c * per * bins, per * bins)
        copies.append(
            (
                pltpu.make_async_copy(t_hbm.at[span, tail, :], t_buf.at[span], sems.at[0, c]),
                pltpu.make_async_copy(s_hbm.at[span, tail, :], s_buf.at[span], sems.at[1, c]),
            )
        )
        for copy in copies[c]:
            copy.start()
    for copy in others[1:]:
        copy.start()
    width = HALO + MAXOFF
    end = out_ref.shape[0]
    row = T + count * width
    last = row + LEFT * levels
    out_ref[0:T, :] = jnp.zeros((T, rows), jnp.float32)
    out_ref[last + MAXOFF : end, :] = jnp.zeros((end - last - MAXOFF, rows), jnp.float32)
    others[0].wait()

    def level_body(level, _):
        unshifted = n_buf[pl.ds(level, 1), :] == 0
        for b in range(bins):
            lb = level * bins + b
            row = T + lb * width
            out_ref[pl.ds(row, HALO), :] = t_buf[lb, T - HALO : T, :]
            first, second = s_buf[lb, T - 2 : T - 1, :], s_buf[lb, T - 1 : T, :]
            out_ref[pl.ds(row + HALO, 1), :] = jnp.where(unshifted, first, second)
            out_ref[pl.ds(row + HALO + 1, 1), :] = second
        return 0

    for c in range(chunks):
        for copy in copies[c]:
            copy.wait()
        lax.fori_loop(c * per, (c + 1) * per, level_body, 0)
    for copy in others[1:]:
        copy.wait()
    for level in range(levels):
        out_ref[row + LEFT * level : row + LEFT * (level + 1), :] = f_buf[level, T - LEFT : T, :]
    out_ref[last : last + MAXOFF, :] = area_buf[T - MAXOFF : T, :]


def interior_kernel(
    t_hbm, s_hbm, f_ref, area_ref, n_ref,
    t0_ref, s0_ref, adv_hbm, seed_hbm, w_ref, ap_ref, red_ref,
    t_buf, s_buf, adv_ref, seed_ref, part, sems, out_sems,
):
    count, columns, _ = t_hbm.shape
    levels = f_ref.shape[0]
    bins = count // levels
    chunks = 4
    per = levels // chunks
    copies = []
    for c in range(chunks):
        span = pl.ds(c * per * bins, per * bins)
        copies.append(
            (
                pltpu.make_async_copy(t_hbm.at[span], t_buf.at[span], sems.at[0, c]),
                pltpu.make_async_copy(s_hbm.at[span], s_buf.at[span], sems.at[1, c]),
            )
        )
        copies[c][0].start()
        copies[c][1].start()

    tiles = range(1, columns // T)

    def copies_out(c):
        span = pl.ds(c * per * bins, per * bins)
        inner = pl.ds(T, columns - T)
        return (
            pltpu.make_async_copy(adv_ref.at[span], adv_hbm.at[span, inner, :], out_sems.at[0, c]),
            pltpu.make_async_copy(seed_ref.at[span], seed_hbm.at[span, inner, :], out_sems.at[1, c]),
        )

    def level_body(level, _):
        shift_is = masks(n_ref, level)
        weights, areas = [], []
        for v in tiles:
            cell = T * v - OFF
            face = pick(lambda r: f_ref[level, pl.ds(r, T), :], cell, shift_is)
            west = pick(lambda r: f_ref[level, pl.ds(r, T), :], cell - 1, shift_is)
            area = pick(lambda r: area_ref[pl.ds(r, T), :], cell, shift_is)
            w = tap_weights(face, west, 1.0 / area, shift_is)
            for k, value in enumerate(w):
                w_ref[level, k, pl.ds(T * v, T), :] = value
            ap_ref[level, pl.ds(T * v, T), :] = area
            weights.append(w)
            areas.append(area)

        def bin_body(b, _):
            lb = level * bins + b
            mass = None
            for v in range(columns // T):
                value = t_buf[lb, T * v : T * v + T, :]
                if v == 0:
                    t0_ref[lb, T : 2 * T, :] = value
                value = area_ref[T * v : T * v + T, :] * value
                mass = value if mass is None else mass + value
            early = pick_first(lambda r: s_buf[lb, pl.ds(r, T), :], shift_is)
            s0_ref[lb] = early
            after = dot = None
            for v, w, area in zip(tiles, weights, areas):
                cell = T * v - OFF
                advected = fir(w, lambda r: t_buf[lb, pl.ds(r, T), :], cell - LEFT)
                adv_ref[lb, pl.ds(T * v - T, T), :] = advected
                positive, _ = floor_parts(advected)
                seed = pick(lambda r: s_buf[lb, pl.ds(r, T), :], cell, shift_is)
                seed_ref[lb, pl.ds(T * v - T, T), :] = seed
                after = area * positive if after is None else after + area * positive
                dot = seed * positive if dot is None else dot + seed * positive
            for k, value in enumerate((mass, after, dot)):
                part[k, pl.ds(lb * T, T), :] = value
            return 0

        lax.fori_loop(0, bins, bin_body, 0, unroll=True)
        return 0

    for c in range(chunks):
        copies[c][0].wait()
        copies[c][1].wait()
        lax.fori_loop(c * per, (c + 1) * per, level_body, 0)
        for copy in copies_out(c):
            copy.start()
    reduce_rows(part, red_ref, 3, count)

    for c in range(chunks):
        for copy in copies_out(c):
            copy.wait()


def reduce_rows(part, red_ref, kinds, count):
    def body(g, _):
        for k in range(kinds):
            total = part[k, pl.ds(g * T * T, T, stride=T), :]
            for s in range(1, T):
                total = total + part[k, pl.ds(g * T * T + s, T, stride=T), :]
            red_ref[k, pl.ds(g * T, T), :] = total
        return 0

    lax.fori_loop(0, count // T, body, 0, unroll=5)


def left_kernel(
    m_ref, t0_in, s0_in, w_in, ap_in, adv_in, seed_in, red_ref, f_ref, area_ref, n_ref,
    t0_ref, w_ref, ap_ref, adv_hbm, seed_hbm, sum_ref, adv_out,
    adv_ref, seed_ref, part, red_new, f_buf, area_buf, sems,
):
    count = t0_ref.shape[0]
    levels, _, rows = f_ref.shape
    bins = count // levels
    width = HALO + MAXOFF
    f_row = T + count * width
    area_row = f_row + LEFT * levels
    area_buf[0:T, :] = m_ref[area_row - (T - MAXOFF) : area_row + MAXOFF, :]
    area_buf[T : 2 * T, :] = area_ref[0:T, :]
    cell = T - OFF
    sublane = lax.broadcasted_iota(jnp.int32, (T, rows), 0)
    chunks = sems.shape[1]
    per = levels // chunks
    copies = []
    for c in range(chunks):
        span = pl.ds(c * per * bins, per * bins)
        copies.append(
            (
                pltpu.make_async_copy(adv_ref.at[span], adv_hbm.at[span, pl.ds(0, T), :], sems.at[0, c]),
                pltpu.make_async_copy(seed_ref.at[span], seed_hbm.at[span, pl.ds(0, T), :], sems.at[1, c]),
            )
        )

    def level_body(level, _):
        shift_is = masks(n_ref, level)
        remote = sublane + jnp.broadcast_to(n_ref[pl.ds(level, 1), :], (T, rows)) < OFF
        f_buf[level, 0:T, :] = m_ref[pl.ds(f_row + LEFT * level - (T - LEFT), T), :]
        f_buf[level, T : 2 * T, :] = f_ref[level, 0:T, :]
        face = pick(lambda r: f_buf[level, pl.ds(r, T), :], cell, shift_is)
        west = pick(lambda r: f_buf[level, pl.ds(r, T), :], cell - 1, shift_is)
        area = pick(lambda r: area_buf[pl.ds(r, T), :], cell, shift_is)
        w = tap_weights(face, west, 1.0 / area, shift_is)
        for k, value in enumerate(w):
            w_ref[level, k, 0:T, :] = value
        ap_ref[level, 0:T, :] = area

        for b in range(bins):
            lb = level * bins + b
            t0_ref[lb, 0:T, :] = m_ref[pl.ds(T + lb * width - (T - HALO), T), :]
        for b in range(bins):
            lb = level * bins + b
            advected = fir(w, lambda r: t0_ref[lb, pl.ds(r, T), :], cell - LEFT)
            adv_ref[lb] = advected
            positive, _ = floor_parts(advected)
            seed = jnp.where(remote, m_ref[pl.ds(T + lb * width + HALO, T), :], s0_in[lb])
            seed_ref[lb] = seed
            part[0, pl.ds(lb * T, T), :] = area * positive
            part[1, pl.ds(lb * T, T), :] = seed * positive
            adv_out[pl.ds(lb * HALO, HALO), :] = advected[0:HALO]
        return 0

    for c in range(chunks):
        lax.fori_loop(c * per, (c + 1) * per, level_body, 0)
        for copy in copies[c]:
            copy.start()
    row = count * HALO
    for level in range(levels):
        adv_out[row + HALO * level : row + HALO * (level + 1), :] = f_ref[level, 0:HALO, :]
    row = row + HALO * levels
    adv_out[row : row + HALO, :] = area_ref[0:HALO, :]
    end = adv_out.shape[0]
    adv_out[row + HALO : end, :] = jnp.zeros((end - row - HALO, rows), jnp.float32)
    reduce_rows(part, red_new, 2, count)
    ones = jnp.ones((T, rows), jnp.float32)
    for k in range(3):
        values = red_ref[k] if k == 0 else red_ref[k] + red_new[k - 1]
        total = lax.dot_general(
            ones, values, (((1,), (1,)), ((), ())), precision=HIGHEST, preferred_element_type=jnp.float32
        )
        for peer in range(sum_ref.shape[0]):
            sum_ref[peer, k : k + 1, :] = total[0:1, :]
    for c in range(chunks):
        for copy in copies[c]:
            copy.wait()


def pack_left_kernel(seed_hbm, out_ref, seed_ref, sem):
    count, _, rows = seed_ref.shape
    copy = pltpu.make_async_copy(seed_hbm.at[:, pl.ds(0, T), :], seed_ref, sem)
    copy.start()
    start, end = count * HALO, out_ref.shape[0]
    out_ref[start:end, :] = jnp.zeros((end - start, rows), jnp.float32)
    copy.wait()

    def body(lb, _):
        out_ref[pl.ds(lb * HALO, HALO), :] = seed_ref[lb, 0:HALO, :]
        return 0

    lax.fori_loop(0, count, body, 0, unroll=15)


def main_kernel(
    g_ref, m_ref, adv_hbm, seed_hbm, w_in, ap_in, f_ref, area_ref, n_ref,
    next_hbm, adj_hbm, scale_ref, s_last, gain_ref, loss_ref, w_ref,
    s_buf, p_buf, a_buf, seed_ref, next_buf, adj_buf, f_buf, area_buf, sems, in_sems,
):
    count, rows = scale_ref.shape[1:]
    levels, columns, _ = f_ref.shape
    bins = count // levels
    peers = g_ref.shape[0]
    tiles = columns // T
    last = columns - T
    chunks = 4
    per = levels // chunks
    copies_in = []
    for c in range(chunks):
        span = pl.ds(c * per * bins, per * bins)
        copies_in.append(
            (
                pltpu.make_async_copy(adv_hbm.at[span], a_buf.at[span], in_sems.at[0, c]),
                pltpu.make_async_copy(seed_hbm.at[span], seed_ref.at[span], in_sems.at[1, c]),
            )
        )
        copies_in[c][0].start()
        copies_in[c][1].start()
    ones = jnp.ones((peers, rows), jnp.float32)
    sums = [
        lax.dot_general(
            g_ref[:, k, :], ones, (((0,), (0,)), ((), ())), precision=HIGHEST, preferred_element_type=jnp.float32
        )
        for k in range(3)
    ]
    mass_before, mass_after, seed_dot = sums
    direct = seed_dot / mass_after
    rescale = mass_before / mass_after
    scale_ref[0] = rescale
    scale_ref[1] = rescale * direct
    scale_ref[2] = direct

    f_row = count * HALO
    area_row = f_row + HALO * levels
    area_buf[0:T, :] = area_ref[last:columns, :]
    area_buf[T : 2 * T, :] = m_ref[area_row : area_row + T, :]

    def copies(c):
        span = pl.ds(c * per * bins, per * bins)
        return (
            pltpu.make_async_copy(next_buf.at[span], next_hbm.at[span], sems.at[0, c]),
            pltpu.make_async_copy(adj_buf.at[span], adj_hbm.at[span, pl.ds(0, last), :], sems.at[1, c]),
        )

    def level_body(level, _):
        shift_is = masks(n_ref, level)
        f_buf[level, 0:T, :] = f_ref[level, last:columns, :]
        f_buf[level, T : 2 * T, :] = m_ref[pl.ds(f_row + HALO * level, T), :]
        cell = T - OFF
        face = pick(lambda r: f_buf[level, pl.ds(r, T), :], cell, shift_is)
        west = pick(lambda r: f_buf[level, pl.ds(r, T), :], cell - 1, shift_is)
        area = pick(lambda r: area_buf[pl.ds(r, T), :], cell, shift_is)
        for k, value in enumerate(tap_weights(face, west, 1.0 / area, shift_is)):
            w_ref[level, k, columns : columns + T, :] = value
        areas = [ap_in[level, T * v : T * v + T, :] for v in range(tiles)]

        def seed_body(b, _):
            lb = level * bins + b
            rescale = scale_ref[0, pl.ds(lb, 1), :]
            feedback = scale_ref[1, pl.ds(lb, 1), :]
            for v in range(tiles):
                positive, ratio = floor_parts(a_buf[lb, T * v : T * v + T, :])
                p_buf[b, T * v : T * v + T, :] = positive
                seed = seed_ref[lb, T * v : T * v + T, :]
                value = (rescale * seed - feedback * areas[v]) * ratio
                s_buf[b, T * v : T * v + T, :] = value
                if v == tiles - 1:
                    s_last[lb, 0:T, :] = value
            positive, ratio = floor_parts(m_ref[pl.ds(lb * HALO, T), :])
            p_buf[b, columns : columns + T, :] = positive
            gain_ref[lb] = rescale * ratio
            loss_ref[lb] = (feedback * area) * ratio
            return 0

        lax.fori_loop(0, bins, seed_body, 0, unroll=True)
        weights = [
            [w_ref[level, k, pl.ds(T * q + OFF + LEFT - k, T), :] for k in range(LEFT + RIGHT + 1)]
            for q in range(tiles - 1)
        ]

        def bin_body(b, _):
            lb = level * bins + b
            rescale = scale_ref[0, pl.ds(lb, 1), :]
            direct = scale_ref[2, pl.ds(lb, 1), :]
            for q in range(tiles):
                if q < tiles - 1:
                    total = area_ref[T * q : T * q + T, :] * direct
                    for k in range(LEFT + RIGHT + 1):
                        total = total + weights[q][k] * s_buf[b, pl.ds(T * q + OFF + LEFT - k, T), :]
                    adj_buf[lb, T * q : T * q + T, :] = total
                positive = pick_back(lambda r: p_buf[b, pl.ds(r, T), :], T * q + OFF, shift_is)
                next_buf[lb, T * q : T * q + T, :] = positive * rescale
            return 0

        lax.fori_loop(0, bins, bin_body, 0, unroll=True)
        return 0

    for c in range(chunks):
        copies_in[c][0].wait()
        copies_in[c][1].wait()
        lax.fori_loop(c * per, (c + 1) * per, level_body, 0)
        for copy in copies(c):
            copy.start()
    for c in range(chunks):
        for copy in copies(c):
            copy.wait()


def right_kernel(
    m_ref, gain_ref, loss_ref, s_in, w_ref, scale_ref, area_ref, adj_in,
    adj_hbm, s_ref,
    adj_buf, sems,
):
    count = adj_buf.shape[0]
    levels = w_ref.shape[0]
    bins = count // levels
    columns = area_ref.shape[0]
    last = columns - T
    parts = in_chunks(levels, sems.shape[0])

    def copy_of(c):
        span = pl.ds(parts[c][0] * bins, (parts[c][1] - parts[c][0]) * bins)
        return pltpu.make_async_copy(adj_buf.at[span], adj_hbm.at[span, pl.ds(last, T), :], sems.at[c])

    def level_body(level, _):
        for b in range(bins):
            lb = level * bins + b
            s_ref[lb, T : 2 * T, :] = gain_ref[lb] * m_ref[pl.ds(lb * HALO, T), :] - loss_ref[lb]
        weights = [w_ref[level, k, pl.ds(last + OFF + LEFT - k, T), :] for k in range(LEFT + RIGHT + 1)]
        area = area_ref[last:columns, :]
        for b in range(bins):
            lb = level * bins + b
            total = area * scale_ref[2, pl.ds(lb, 1), :]
            for k in range(LEFT + RIGHT + 1):
                total = total + weights[k] * s_ref[lb, pl.ds(OFF + LEFT - k, T), :]
            adj_buf[lb] = total
        return 0

    for c, (start, end) in enumerate(parts):
        lax.fori_loop(start, end, level_body, 0)
        copy_of(c).start()
    for c in range(len(parts)):
        copy_of(c).wait()


def padded(rows):
    return (rows + 2 * T - 1) // T * T


def shards(tracer, courant_frac, departure_shift, cell_area, adjoint_seed):
    levels, bins, columns, rows = tracer.shape
    count = levels * bins
    f32 = jnp.float32
    tile = lax.axis_size("tile")
    to_right = [(i, (i + 1) % tile) for i in range(tile)]
    to_left = [(target, source) for source, target in to_right]
    hbm = pl.BlockSpec(memory_space=pl.ANY)
    vmem = pl.BlockSpec(memory_space=pltpu.VMEM)
    params = pltpu.CompilerParams(vmem_limit_bytes=VMEM_LIMIT)
    dma = pltpu.SemaphoreType.DMA
    taps = LEFT + RIGHT + 1

    def held(x):
        return pltpu.with_memory_space_constraint(x, pltpu.VMEM)

    def far(x):
        return pltpu.with_memory_space_constraint(x, pltpu.HBM)

    def cost(flops, nbytes):
        return pl.CostEstimate(flops=flops, bytes_accessed=nbytes, transcendentals=0)

    size = 4 * count * columns * rows
    t = tracer.reshape(count, columns, rows)
    seed = adjoint_seed.reshape(count, columns, rows)

    message = pl.pallas_call(
        pack_right_kernel,
        out_shape=jax.ShapeDtypeStruct((padded(T + count * (HALO + MAXOFF) + LEFT * levels + MAXOFF), rows), f32),
        in_specs=[hbm] * 5,
        out_specs=vmem,
        scratch_shapes=[
            pltpu.VMEM((count, T, rows), f32),
            pltpu.VMEM((count, T, rows), f32),
            pltpu.VMEM((levels, T, rows), f32),
            pltpu.VMEM((T, rows), f32),
            pltpu.VMEM((levels, rows), jnp.int32),
            dma((2, 4)),
            dma((3,)),
        ],
        compiler_params=params,
        cost_estimate=cost(0, size),
        name="pack_right",
    )(far(t), far(seed), far(courant_frac), far(cell_area), far(departure_shift))
    from_left = lax.ppermute(message, "tile", to_right)

    t0, s0, adv, seeds, w, ap, red = pl.pallas_call(
        interior_kernel,
        out_shape=(
            pltpu.VMEM((count, 2 * T, rows), f32),
            pltpu.VMEM((count, T, rows), f32),
            pltpu.HBM((count, columns, rows), f32),
            pltpu.HBM((count, columns, rows), f32),
            pltpu.VMEM((levels, taps, columns + T, rows), f32),
            pltpu.VMEM((levels, columns + T, rows), f32),
            pltpu.VMEM((3, count, rows), f32),
        ),
        in_specs=[hbm, hbm, vmem, vmem, vmem],
        out_specs=(vmem, vmem, hbm, hbm, vmem, vmem, vmem),
        scratch_shapes=[
            pltpu.VMEM((count, columns, rows), f32),
            pltpu.VMEM((count, columns, rows), f32),
            pltpu.VMEM((count, columns - T, rows), f32),
            pltpu.VMEM((count, columns - T, rows), f32),
            pltpu.VMEM((3, count * T, rows), f32),
            dma((2, 4)),
            dma((2, 4)),
        ],
        compiler_params=params,
        cost_estimate=cost(30 * size, 4 * size),
        name="interior",
    )(far(t), far(seed), courant_frac, cell_area, departure_shift)

    _, w, ap, adv, seeds, sums, adv_left = pl.pallas_call(
        left_kernel,
        out_shape=(
            pltpu.VMEM(t0.shape, f32),
            pltpu.VMEM(w.shape, f32),
            pltpu.VMEM(ap.shape, f32),
            pltpu.HBM(adv.shape, f32),
            pltpu.HBM(seeds.shape, f32),
            jax.ShapeDtypeStruct((tile, 3, count), f32),
            jax.ShapeDtypeStruct((padded(count * HALO + HALO * levels + HALO), rows), f32),
        ),
        in_specs=[vmem] * 5 + [hbm] * 2 + [vmem] * 4,
        out_specs=(vmem,) * 3 + (hbm,) * 2 + (vmem,) * 2,
        input_output_aliases={1: 0, 3: 1, 4: 2, 5: 3, 6: 4},
        scratch_shapes=[
            pltpu.VMEM((count, T, rows), f32),
            pltpu.VMEM((count, T, rows), f32),
            pltpu.VMEM((2, count * T, rows), f32),
            pltpu.VMEM((2, count, rows), f32),
            pltpu.VMEM((levels, 2 * T, rows), f32),
            pltpu.VMEM((2 * T, rows), f32),
            dma((2, 4)),
        ],
        compiler_params=params,
        cost_estimate=cost(10 * size, size),
        name="left_edge",
    )(
        from_left, held(t0), held(s0), held(w), held(ap), far(adv), far(seeds), held(red),
        courant_frac, cell_area, departure_shift,
    )

    adv_right = lax.ppermute(adv_left, "tile", to_left)
    sums = lax.all_to_all(sums, "tile", 0, 0)
    seed_left = pl.pallas_call(
        pack_left_kernel,
        out_shape=jax.ShapeDtypeStruct((padded(count * HALO), rows), f32),
        in_specs=[hbm],
        out_specs=vmem,
        scratch_shapes=[pltpu.VMEM((count, T, rows), f32), dma],
        compiler_params=params,
        cost_estimate=cost(size, size),
        name="pack_left",
    )(far(seeds))
    seed_right = lax.ppermute(seed_left, "tile", to_left)

    tracer_next, tracer_adjoint, scale, s_last, gain, loss, w = pl.pallas_call(
        main_kernel,
        out_shape=(
            jax.ShapeDtypeStruct((count, columns, rows), f32),
            jax.ShapeDtypeStruct((count, columns, rows), f32),
            pltpu.VMEM((3, count, rows), f32),
            pltpu.VMEM((count, 2 * T, rows), f32),
            pltpu.VMEM((count, T, rows), f32),
            pltpu.VMEM((count, T, rows), f32),
            pltpu.VMEM(w.shape, f32),
        ),
        in_specs=[vmem] * 2 + [hbm] * 2 + [vmem] * 5,
        out_specs=(hbm, hbm) + (vmem,) * 5,
        input_output_aliases={4: 6},
        scratch_shapes=[
            pltpu.VMEM((bins, columns, rows), f32),
            pltpu.VMEM((bins, columns + T, rows), f32),
            pltpu.VMEM((count, columns, rows), f32),
            pltpu.VMEM((count, columns, rows), f32),
            pltpu.VMEM((count, columns, rows), f32),
            pltpu.VMEM((count, columns - T, rows), f32),
            pltpu.VMEM((levels, 2 * T, rows), f32),
            pltpu.VMEM((2 * T, rows), f32),
            dma((2, 4)),
            dma((2, 4)),
        ],
        compiler_params=params,
        cost_estimate=cost(MAIN_FLOPS * size, 4 * size),
        name="main_part",
    )(
        sums, adv_right, far(adv), far(seeds), held(w), held(ap),
        courant_frac, cell_area, departure_shift,
    )

    tracer_adjoint, _ = pl.pallas_call(
        right_kernel,
        out_shape=(jax.ShapeDtypeStruct((count, columns, rows), f32), pltpu.VMEM(s_last.shape, f32)),
        in_specs=[vmem] * 7 + [hbm],
        out_specs=(hbm, vmem),
        input_output_aliases={7: 0, 3: 1},
        scratch_shapes=[pltpu.VMEM((count, T, rows), f32), dma((4,))],
        compiler_params=params,
        cost_estimate=cost(10 * size, size),
        name="right_edge",
    )(seed_right, held(gain), held(loss), held(s_last), held(w), held(scale), cell_area, tracer_adjoint)
    return tracer_next.reshape(tracer.shape), tracer_adjoint.reshape(tracer.shape)


def solution(mesh):
    return jax.shard_map(
        shards,
        mesh=mesh,
        in_specs=(
            P("group", None, "tile", None),
            P("group", "tile", None),
            P("group", None),
            P("tile", None),
            P("group", None, "tile", None),
        ),
        out_specs=(P("group", None, "tile", None), P("group", None, "tile", None)),
        check_vma=False,
    )
```

```python
import jax
import jax.numpy as jnp
from jax import lax
from jax.experimental import pallas as pl
from jax.experimental.pallas import tpu as pltpu
from jax.sharding import PartitionSpec as P

MAXOFF = 2
FLOOR2 = 0.1 * 0.1
LEFT, RIGHT = 3, 2
OFF = MAXOFF
HALO = LEFT + MAXOFF
T = 8
LANES = 128
VMEM_LIMIT = 20 * 2**20
CHUNKS = 8
HIGHEST = lax.Precision.HIGHEST


def tap_weights(face, west, inverse, shift_is):
    def taps(f):
        f2 = f * f
        f3 = f2 * f
        alpha = 3.0 * f2 - 2.0 * f3
        beta = f3 - f2
        gamma = f - 2.0 * f2 + f3
        return (
            beta * (-1.0 / 12.0),
            (7.0 / 12.0) * beta - (1.0 / 12.0) * gamma,
            alpha + (7.0 / 12.0) * (beta + gamma),
            (7.0 / 12.0) * gamma - (1.0 / 12.0) * beta,
            gamma * (-1.0 / 12.0),
        )

    east_taps, west_taps = taps(face), taps(west)
    weights = [west_taps[0] * inverse]
    for k in range(4):
        weights.append((west_taps[k + 1] - east_taps[k]) * inverse)
    weights.append(-east_taps[4] * inverse)
    is0, is1, is2 = shift_is
    rest = 1.0 - inverse
    weights[3] = weights[3] + jnp.where(is0, 1.0, inverse)
    weights[4] = weights[4] + jnp.where(is1, rest, 0.0)
    weights[5] = weights[5] + jnp.where(is2, rest, 0.0)
    return weights


def masks(shift_ref, level):
    n = jnp.broadcast_to(shift_ref[pl.ds(level, 1), :], (T, shift_ref.shape[1]))
    return n == 0, n == 1, n == 2


def pick(load, start, shift_is):
    return jnp.where(
        shift_is[0], load(start), jnp.where(shift_is[1], load(start + 1), load(start + 2))
    )


def pick_back(load, start, shift_is):
    return jnp.where(
        shift_is[0], load(start), jnp.where(shift_is[1], load(start - 1), load(start - 2))
    )


def pick_first(load, shift_is):
    first = load(0)
    two_down = jnp.concatenate([first[T - 2 : T], first[0 : T - 2]], axis=0)
    one_down = jnp.concatenate([first[T - 1 : T], first[0 : T - 1]], axis=0)
    return jnp.where(shift_is[0], two_down, jnp.where(shift_is[1], one_down, first))


def pick_last(load, shift_is):
    first = load(0)
    two_up = jnp.concatenate([first[T - 2 : T], first[0 : T - 2]], axis=0)
    one_up = jnp.concatenate([first[T - 1 : T], first[0 : T - 1]], axis=0)
    return jnp.where(shift_is[0], two_up, one_up)


def fir(weights, load, start):
    total = weights[0] * load(start)
    for k in range(1, LEFT + RIGHT + 1):
        total = total + weights[k] * load(start + k)
    return total


def floor_parts(advected):
    square = advected * advected + FLOOR2
    root = lax.rsqrt(square)
    return square * root, advected * root


def pack_right_kernel(t_hbm, s_hbm, f_hbm, area_hbm, n_hbm, out_ref, t_buf, s_buf, f_buf, area_buf, n_buf, sems, small):
    count, columns, rows = t_hbm.shape
    levels = f_hbm.shape[0]
    bins = count // levels
    chunks = sems.shape[1]
    per = levels // chunks
    t_rows, s_rows = t_buf.shape[1], s_buf.shape[1]

    def copies(c):
        span = pl.ds(c * per * bins, per * bins)
        return (
            pltpu.make_async_copy(t_hbm.at[span, pl.ds(columns - t_rows, t_rows), :], t_buf.at[span], sems.at[0, c]),
            pltpu.make_async_copy(s_hbm.at[span, pl.ds(columns - s_rows, s_rows), :], s_buf.at[span], sems.at[1, c]),
        )

    others = [
        pltpu.make_async_copy(n_hbm, n_buf, small.at[0]),
        pltpu.make_async_copy(f_hbm.at[:, pl.ds(columns - T, T), :], f_buf, small.at[1]),
        pltpu.make_async_copy(area_hbm.at[pl.ds(columns - T, T), :], area_buf, small.at[2]),
    ]
    others[0].start()
    for c in range(chunks):
        for copy in copies(c):
            copy.start()
    for copy in others[1:]:
        copy.start()
    width = HALO + MAXOFF
    end = out_ref.shape[0]
    row = T + count * width
    last = row + LEFT * levels
    out_ref[0:T, :] = jnp.zeros((T, rows), jnp.float32)
    out_ref[last + MAXOFF : end, :] = jnp.zeros((end - last - MAXOFF, rows), jnp.float32)
    others[0].wait()

    def level_body(level, _):
        @pl.when(level % per == 0)
        def _():
            for copy in copies(level // per):
                copy.wait()

        unshifted = n_buf[pl.ds(level, 1), :] == 0

        def bin_body(b, _):
            lb = level * bins + b
            row = T + lb * width
            out_ref[pl.ds(row, HALO), :] = t_buf[lb, t_rows - HALO : t_rows, :]
            second = s_buf[lb, s_rows - 1 : s_rows, :]
            out_ref[pl.ds(row + HALO, 1), :] = jnp.where(unshifted, s_buf[lb, s_rows - 2 : s_rows - 1, :], second)
            out_ref[pl.ds(row + HALO + 1, 1), :] = second
            return 0

        lax.fori_loop(0, bins, bin_body, 0, unroll=15)
        return 0

    lax.fori_loop(0, levels, level_body, 0)
    for copy in others[1:]:
        copy.wait()
    for level in range(levels):
        out_ref[row + LEFT * level : row + LEFT * (level + 1), :] = f_buf[level, T - LEFT : T, :]
    out_ref[last : last + MAXOFF, :] = area_buf[T - MAXOFF : T, :]


def shifted_weights(f_of, area_of, cell, shift_is):
    face = pick(f_of, cell, shift_is)
    west = pick(f_of, cell - 1, shift_is)
    area = pick(area_of, cell, shift_is)
    return area, tap_weights(face, west, 1.0 / area, shift_is)


def each_chunk(level, per, act):
    @pl.when(level % per == 0)
    def _():
        act(level // per)


def interior_kernel(
    t_hbm, s_hbm, f_ref, area_ref, n_ref,
    t0_ref, s0_ref, t2_ref, s2_ref, ratio_ref, pos_ref, seed_ref, w_ref, ap_ref, red_ref, out_ref,
    t_buf, s_buf, part, in_sems,
):
    count, columns, rows = t_hbm.shape
    levels = f_ref.shape[0]
    bins = count // levels
    chunks = in_sems.shape[1]
    per = levels // chunks
    tiles = range(1, columns // T)
    last = columns - T
    width = 2 * HALO

    def copies_in(c):
        span = pl.ds(c * per * bins, per * bins)
        return (
            pltpu.make_async_copy(t_hbm.at[span], t_buf.at[span], in_sems.at[0, c]),
            pltpu.make_async_copy(s_hbm.at[span], s_buf.at[span], in_sems.at[1, c]),
        )

    for c in range(chunks):
        for copy in copies_in(c):
            copy.start()
    row = count * width
    for level in range(levels):
        out_ref[row + HALO * level : row + HALO * (level + 1), :] = f_ref[level, 0:HALO, :]
    row = row + HALO * levels
    out_ref[row : row + HALO, :] = area_ref[0:HALO, :]
    end = out_ref.shape[0]
    out_ref[row + HALO : end, :] = jnp.zeros((end - row - HALO, rows), jnp.float32)

    def level_body(level, _):
        def arrive(c):
            for copy in copies_in(c):
                copy.wait()

        each_chunk(level, per, arrive)
        shift_is = masks(n_ref, level)
        own = []
        for v in tiles:
            area, w = shifted_weights(
                lambda r: f_ref[level, pl.ds(r, T), :], lambda r: area_ref[pl.ds(r, T), :], T * v - OFF, shift_is
            )
            own.append((area, w))
            ap_ref[level, T * v : T * v + T, :] = area
            for k, value in enumerate(w):
                w_ref[level, k, T * v : T * v + T, :] = value
        for b in range(bins):
            lb = level * bins + b
            mass = None
            for v in range(columns // T):
                value = t_buf[lb, T * v : T * v + T, :]
                if v == 0:
                    t0_ref[lb, T : 2 * T, :] = value
                if v == columns // T - 1:
                    t2_ref[lb, 0:T, :] = value
                value = area_ref[T * v : T * v + T, :] * value
                mass = value if mass is None else mass + value
            early = pick_first(lambda r: s_buf[lb, pl.ds(r, T), :], shift_is)
            s0_ref[lb] = early
            s2_ref[lb] = pick_last(lambda r: s_buf[lb, pl.ds(last + r, T), :], shift_is)
            out_ref[pl.ds(lb * width, HALO), :] = t_buf[lb, 0:HALO, :]
            out_ref[pl.ds(lb * width + HALO, HALO), :] = early[0:HALO]
            after = dot = None
            for v, (area, w) in zip(tiles, own):
                cell = T * v - OFF
                advected = fir(w, lambda r: t_buf[lb, pl.ds(r, T), :], cell - LEFT)
                positive, ratio = floor_parts(advected)
                ratio_ref[lb, T * v : T * v + T, :] = ratio
                pos_ref[lb, T * v : T * v + T, :] = positive
                seed = pick(lambda r: s_buf[lb, pl.ds(r, T), :], cell, shift_is)
                seed_ref[lb, T * v : T * v + T, :] = seed
                after = area * positive if after is None else after + area * positive
                dot = seed * positive if dot is None else dot + seed * positive
            for k, value in enumerate((mass, after, dot)):
                part[k, pl.ds(lb * T, T), :] = value
        return 0

    lax.fori_loop(0, levels, level_body, 0)
    reduce_rows(part, red_ref, 3, count)


def reduce_rows(part, red_ref, kinds, count):
    def body(g, _):
        for k in range(kinds):
            total = part[k, pl.ds(g * T * T, T, stride=T), :]
            for s in range(1, T):
                total = total + part[k, pl.ds(g * T * T + s, T, stride=T), :]
            red_ref[k, pl.ds(g * T, T), :] = total
        return 0

    lax.fori_loop(0, count // T, body, 0, unroll=5)
    rest = red_ref.shape[1] - count
    for k in range(kinds):
        red_ref[k, pl.ds(count, rest), :] = jnp.zeros((rest, red_ref.shape[2]), jnp.float32)


def left_kernel(
    m_ref, t0_in, s0_ref, ratio_in, pos_in, seed_in, w_in, ap_in, red_ref, f_ref, area_ref, n_ref,
    t0_ref, ratio_ref, pos_ref, seed_ref, w_ref, ap_ref, sum_ref,
    part, red_new, f_buf, area_buf,
):
    count = t0_ref.shape[0]
    levels, _, rows = f_ref.shape
    bins = count // levels
    width = HALO + MAXOFF
    f_row = T + count * width
    area_row = f_row + LEFT * levels
    area_buf[0:T, :] = m_ref[area_row - (T - MAXOFF) : area_row + MAXOFF, :]
    area_buf[T : 2 * T, :] = area_ref[0:T, :]
    cell = T - OFF
    sublane = lax.broadcasted_iota(jnp.int32, (T, rows), 0)

    def level_body(level, _):
        shift_is = masks(n_ref, level)
        remote = sublane + jnp.broadcast_to(n_ref[pl.ds(level, 1), :], (T, rows)) < OFF
        f_buf[0:T, :] = m_ref[pl.ds(f_row + LEFT * level - (T - LEFT), T), :]
        f_buf[T : 2 * T, :] = f_ref[level, 0:T, :]
        area, w = shifted_weights(
            lambda r: f_buf[pl.ds(r, T), :], lambda r: area_buf[pl.ds(r, T), :], cell, shift_is
        )
        ap_ref[level, 0:T, :] = area
        for k, value in enumerate(w):
            w_ref[level, k, 0:T, :] = value
        for b in range(bins):
            lb = level * bins + b
            t0_ref[lb, 0:T, :] = m_ref[pl.ds(T + lb * width - (T - HALO), T), :]
        for b in range(bins):
            lb = level * bins + b
            advected = fir(w, lambda r: t0_ref[lb, pl.ds(r, T), :], cell - LEFT)
            positive, ratio = floor_parts(advected)
            ratio_ref[lb, 0:T, :] = ratio
            pos_ref[lb, 0:T, :] = positive
            seed = jnp.where(remote, m_ref[pl.ds(T + lb * width + HALO, T), :], s0_ref[lb])
            seed_ref[lb, 0:T, :] = seed
            part[0, pl.ds(lb * T, T), :] = area * positive
            part[1, pl.ds(lb * T, T), :] = seed * positive
        return 0

    lax.fori_loop(0, levels, level_body, 0)
    reduce_rows(part, red_new, 2, count)
    lines = []
    for k in range(3):
        for half in range(2):
            span = pl.ds(half * LANES, LANES)
            values = red_ref[k, span, :]
            if k:
                values = values + red_new[k - 1, span, :]
            lines.append(jnp.sum(values.T, axis=0, keepdims=True))
    lines.append(jnp.zeros((T - len(lines), rows), jnp.float32))
    sum_ref[...] = jnp.broadcast_to(jnp.concatenate(lines, axis=0)[None], sum_ref.shape)


def middle_kernel(
    ratio_ref, pos_in, seed_ref, w_ref, ap_ref, n_ref, sum_in,
    x_ref, y_ref, own_ref, pos_ref, sum_ref,
    x_buf, y_buf,
):
    levels = n_ref.shape[0]
    count = ratio_ref.shape[0]
    bins = count // levels
    tiles = ratio_ref.shape[1] // T
    taps = range(LEFT + RIGHT + 1)

    def level_body(level, _):
        shift_is = masks(n_ref, level)
        areas = [ap_ref[level, T * v : T * v + T, :] for v in range(tiles)]
        for b in range(bins):
            lb = level * bins + b
            for v in range(tiles):
                part = slice(T * v, T * v + T)
                ratio = ratio_ref[lb, part, :]
                x_buf[b, part, :] = seed_ref[lb, part, :] * ratio
                y_buf[b, part, :] = areas[v] * ratio
            x_ref[lb, T * (tiles - 1) : T * tiles, :] = x_buf[b, T * (tiles - 1) : T * tiles, :]
            y_ref[lb, T * (tiles - 1) : T * tiles, :] = y_buf[b, T * (tiles - 1) : T * tiles, :]
        for q in range(tiles - 1):
            weights = [w_ref[level, k, pl.ds(T * q + OFF + LEFT - k, T), :] for k in taps]
            part = slice(T * q, T * q + T)
            for b in range(bins):
                lb = level * bins + b
                for buf, out in ((x_buf, x_ref), (y_buf, y_ref)):
                    total = weights[0] * buf[b, pl.ds(T * q + OFF + LEFT, T), :]
                    for k in taps[1:]:
                        total = total + weights[k] * buf[b, pl.ds(T * q + OFF + LEFT - k, T), :]
                    out[lb, part, :] = total
                own_ref[lb, part, :] = pick_back(lambda r: pos_ref[lb, pl.ds(r, T), :], T * q + OFF, shift_is)
        return 0

    lax.fori_loop(0, levels, level_body, 0)


def final_kernel(
    g_ref, m_ref, t2_in, s2_ref, x_ref, y_ref, own_ref, pos_in, w_ref, f_ref, area_ref, n_ref,
    next_hbm, adj_hbm, t2_ref, pos_ref,
    scale_ref, w_buf, s_buf, next_buf, adj_buf, f_buf, area_buf, out_sems,
):
    count, columns, rows = next_buf.shape
    levels = f_ref.shape[0]
    bins = count // levels
    peers = g_ref.shape[0]
    tiles = columns // T
    last = columns - T
    chunks = out_sems.shape[1]
    per = levels // chunks
    taps = range(LEFT + RIGHT + 1)
    width = 2 * HALO

    def copies_out(c):
        span = pl.ds(c * per * bins, per * bins)
        return (
            pltpu.make_async_copy(next_buf.at[span], next_hbm.at[span], out_sems.at[0, c]),
            pltpu.make_async_copy(adj_buf.at[span], adj_hbm.at[span], out_sems.at[1, c]),
        )

    total = g_ref[0]
    for peer in range(1, peers):
        total = total + g_ref[peer]
    mass_before, mass_after, seed_dot = total[0:2], total[2:4], total[4:6]
    direct = seed_dot / mass_after
    rescale = mass_before / mass_after
    for k, value in enumerate((rescale, rescale * direct, direct)):
        for half in range(2):
            column = jnp.broadcast_to(value[half : half + 1], (LANES, LANES)).T
            scale_ref[k, pl.ds(half * LANES, LANES), :] = column
    f_row = count * width
    area_row = f_row + HALO * levels
    area_buf[0:T, :] = area_ref[last:columns, :]
    area_buf[T : 2 * T, :] = m_ref[area_row : area_row + T, :]
    sublane = lax.broadcasted_iota(jnp.int32, (T, rows), 0)

    def level_body(level, _):
        shift_is = masks(n_ref, level)
        near = sublane + jnp.broadcast_to(n_ref[pl.ds(level, 1), :], (T, rows)) < OFF
        f_buf[0:T, :] = f_ref[level, last:columns, :]
        f_buf[T : 2 * T, :] = m_ref[pl.ds(f_row + HALO * level, T), :]
        area, w = shifted_weights(
            lambda r: f_buf[pl.ds(r, T), :], lambda r: area_buf[pl.ds(r, T), :], T - OFF, shift_is
        )
        for k in taps:
            w_buf[k, 0:T, :] = w_ref[level, k, last:columns, :]
            w_buf[k, T : 2 * T, :] = w[k]
        weights = [w_buf[k, pl.ds(OFF + LEFT - k, T), :] for k in taps]
        for b in range(bins):
            lb = level * bins + b
            t2_ref[lb, T : 2 * T, :] = m_ref[pl.ds(lb * width, T), :]
        for b in range(bins):
            lb = level * bins + b
            rescale = scale_ref[0, pl.ds(lb, 1), :]
            feedback = scale_ref[1, pl.ds(lb, 1), :]
            advected = fir(w, lambda r: t2_ref[lb, pl.ds(r, T), :], T - OFF - LEFT)
            positive, ratio = floor_parts(advected)
            pos_ref[lb, columns : columns + T, :] = positive
            seed = jnp.where(near, s2_ref[lb], m_ref[pl.ds(lb * width + HALO, T), :])
            s_buf[b, 0:T, :] = rescale * x_ref[lb, last:columns, :] - feedback * y_ref[lb, last:columns, :]
            s_buf[b, T : 2 * T, :] = (rescale * seed - feedback * area) * ratio
        for q in range(tiles):
            part = slice(T * q, T * q + T)
            area_own = area_ref[part, :]
            for b in range(bins):
                lb = level * bins + b
                rescale = scale_ref[0, pl.ds(lb, 1), :]
                value = area_own * scale_ref[2, pl.ds(lb, 1), :]
                if q < tiles - 1:
                    value = value + rescale * x_ref[lb, part, :] - scale_ref[1, pl.ds(lb, 1), :] * y_ref[lb, part, :]
                    own = own_ref[lb, part, :]
                else:
                    for k in taps:
                        value = value + weights[k] * s_buf[b, pl.ds(OFF + LEFT - k, T), :]
                    own = pick_back(lambda r: pos_ref[lb, pl.ds(r, T), :], T * q + OFF, shift_is)
                adj_buf[lb, part, :] = value
                next_buf[lb, part, :] = own * rescale

        def leave(c):
            for copy in copies_out(c - 1):
                copy.start()

        each_chunk(level + 1, per, leave)
        return 0

    lax.fori_loop(0, levels, level_body, 0)
    for c in range(chunks):
        for copy in copies_out(c):
            copy.wait()


def padded(rows):
    return (rows + 2 * T - 1) // T * T


def shards(tracer, courant_frac, departure_shift, cell_area, adjoint_seed):
    levels, bins, columns, rows = tracer.shape
    count = levels * bins
    f32 = jnp.float32
    tile = lax.axis_size("tile")
    to_right = [(i, (i + 1) % tile) for i in range(tile)]
    to_left = [(target, source) for source, target in to_right]
    hbm = pl.BlockSpec(memory_space=pl.ANY)
    vmem = pl.BlockSpec(memory_space=pltpu.VMEM)
    params = pltpu.CompilerParams(vmem_limit_bytes=VMEM_LIMIT)
    dma = pltpu.SemaphoreType.DMA
    taps = LEFT + RIGHT + 1

    def held(x):
        return pltpu.with_memory_space_constraint(x, pltpu.VMEM)

    def far(x):
        return pltpu.with_memory_space_constraint(x, pltpu.HBM)

    def cost(flops, nbytes):
        return pl.CostEstimate(flops=flops, bytes_accessed=nbytes, transcendentals=0)

    size = 4 * count * columns * rows
    t = tracer.reshape(count, columns, rows)
    seed = adjoint_seed.reshape(count, columns, rows)

    message = pl.pallas_call(
        pack_right_kernel,
        out_shape=jax.ShapeDtypeStruct((padded(T + count * (HALO + MAXOFF) + LEFT * levels + MAXOFF), rows), f32),
        in_specs=[hbm] * 5,
        out_specs=vmem,
        scratch_shapes=[
            pltpu.VMEM((count, HALO, rows), f32),
            pltpu.VMEM((count, MAXOFF, rows), f32),
            pltpu.VMEM((levels, T, rows), f32),
            pltpu.VMEM((T, rows), f32),
            pltpu.VMEM((levels, rows), jnp.int32),
            dma((2, 2)),
            dma((3,)),
        ],
        compiler_params=params,
        cost_estimate=cost(0, size),
        name="pack_right",
    )(far(t), far(seed), far(courant_frac), far(cell_area), far(departure_shift))
    from_left = lax.ppermute(message, "tile", to_right)

    strip = pltpu.VMEM((count, T, rows), f32)
    two_strips = pltpu.VMEM((count, 2 * T, rows), f32)
    whole = pltpu.VMEM((count, columns, rows), f32)
    wide = pltpu.VMEM((count, columns + T, rows), f32)
    w_shape = pltpu.VMEM((levels, taps, columns, rows), f32)
    ap_shape = pltpu.VMEM((levels, columns, rows), f32)
    left_rows = padded(2 * count * HALO + HALO * levels + HALO)

    t0, s0, t2, s2, ratio, positive, seeds, w, ap, red, message_left = pl.pallas_call(
        interior_kernel,
        out_shape=(
            two_strips, strip, two_strips, strip, whole, wide, whole, w_shape, ap_shape,
            pltpu.VMEM((3, 2 * LANES, rows), f32),
            jax.ShapeDtypeStruct((left_rows, rows), f32),
        ),
        in_specs=[hbm, hbm, vmem, vmem, vmem],
        out_specs=(vmem,) * 11,
        scratch_shapes=[
            pltpu.VMEM((count, columns, rows), f32),
            pltpu.VMEM((count, columns, rows), f32),
            pltpu.VMEM((3, count * T, rows), f32),
            dma((2, CHUNKS)),
        ],
        compiler_params=params,
        cost_estimate=cost(30 * size, 4 * size),
        name="interior",
    )(far(t), far(seed), courant_frac, cell_area, departure_shift)

    from_left, message_left = lax.optimization_barrier((from_left, message_left))
    from_right = lax.ppermute(message_left, "tile", to_left)

    _, ratio, positive, seeds, w, ap, sums = pl.pallas_call(
        left_kernel,
        out_shape=(
            two_strips, whole, wide, whole, w_shape, ap_shape,
            pltpu.VMEM((tile, T, LANES), f32),
        ),
        in_specs=[vmem] * 12,
        out_specs=(vmem,) * 7,
        input_output_aliases={1: 0, 3: 1, 4: 2, 5: 3, 6: 4, 7: 5},
        scratch_shapes=[
            pltpu.VMEM((2, count * T, rows), f32),
            pltpu.VMEM((2, 2 * LANES, rows), f32),
            pltpu.VMEM((2 * T, rows), f32),
            pltpu.VMEM((2 * T, rows), f32),
        ],
        compiler_params=params,
        cost_estimate=cost(10 * size, size),
        name="left_edge",
    )(
        from_left, held(t0), held(s0), held(ratio), held(positive), held(seeds), held(w), held(ap), held(red),
        courant_frac, cell_area, departure_shift,
    )

    x, y, own, positive, sums = pl.pallas_call(
        middle_kernel,
        out_shape=(whole, whole, two_strips, wide, pltpu.VMEM((tile, T, LANES), f32)),
        in_specs=[vmem] * 7,
        out_specs=(vmem,) * 5,
        input_output_aliases={1: 3, 6: 4},
        scratch_shapes=[pltpu.VMEM((bins, columns, rows), f32), pltpu.VMEM((bins, columns, rows), f32)],
        compiler_params=params,
        cost_estimate=cost(30 * size, size),
        name="middle",
    )(held(ratio), held(positive), held(seeds), held(w), held(ap), departure_shift, held(sums))

    sums = lax.all_to_all(sums, "tile", 0, 0)

    tracer_next, tracer_adjoint, _, _ = pl.pallas_call(
        final_kernel,
        out_shape=(
            jax.ShapeDtypeStruct((count, columns, rows), f32),
            jax.ShapeDtypeStruct((count, columns, rows), f32),
            two_strips,
            wide,
        ),
        in_specs=[vmem] * 12,
        out_specs=(hbm, hbm, vmem, vmem),
        input_output_aliases={2: 2, 7: 3},
        scratch_shapes=[
            pltpu.VMEM((3, 2 * LANES, rows), f32),
            pltpu.VMEM((taps, 2 * T, rows), f32),
            pltpu.VMEM((bins, 2 * T, rows), f32),
            pltpu.VMEM((count, columns, rows), f32),
            pltpu.VMEM((count, columns, rows), f32),
            pltpu.VMEM((2 * T, rows), f32),
            pltpu.VMEM((2 * T, rows), f32),
            dma((2, CHUNKS)),
        ],
        compiler_params=params,
        cost_estimate=cost(10 * size, size),
        name="final",
    )(
        sums, from_right, held(t2), held(s2), held(x), held(y), held(own), held(positive), held(w),
        courant_frac, cell_area, departure_shift,
    )
    return tracer_next.reshape(tracer.shape), tracer_adjoint.reshape(tracer.shape)


def solution(mesh):
    return jax.shard_map(
        shards,
        mesh=mesh,
        in_specs=(
            P("group", None, "tile", None),
            P("group", "tile", None),
            P("group", None),
            P("tile", None),
            P("group", None, "tile", None),
        ),
        out_specs=(P("group", None, "tile", None), P("group", None, "tile", None)),
        check_vma=False,
    )
```

```python
import jax
import jax.numpy as jnp
from jax import lax
from jax.experimental import pallas as pl
from jax.experimental.pallas import tpu as pltpu
from jax.sharding import PartitionSpec as P

MAXOFF = 2
FLOOR2 = 0.1 * 0.1
LEFT, RIGHT = 3, 2
OFF = MAXOFF
HALO = LEFT + MAXOFF
T = 8
LANES = 128
VMEM_LIMIT = 20 * 2**20
CHUNKS = 4
HIGHEST = lax.Precision.HIGHEST


def tap_weights(face, west, inverse, shift_is):
    def taps(f):
        f2 = f * f
        f3 = f2 * f
        alpha = 3.0 * f2 - 2.0 * f3
        beta = f3 - f2
        gamma = f - 2.0 * f2 + f3
        return (
            beta * (-1.0 / 12.0),
            (7.0 / 12.0) * beta - (1.0 / 12.0) * gamma,
            alpha + (7.0 / 12.0) * (beta + gamma),
            (7.0 / 12.0) * gamma - (1.0 / 12.0) * beta,
            gamma * (-1.0 / 12.0),
        )

    east_taps, west_taps = taps(face), taps(west)
    weights = [west_taps[0] * inverse]
    for k in range(4):
        weights.append((west_taps[k + 1] - east_taps[k]) * inverse)
    weights.append(-east_taps[4] * inverse)
    is0, is1, is2 = shift_is
    rest = 1.0 - inverse
    weights[3] = weights[3] + jnp.where(is0, 1.0, inverse)
    weights[4] = weights[4] + jnp.where(is1, rest, 0.0)
    weights[5] = weights[5] + jnp.where(is2, rest, 0.0)
    return weights


def masks(shift_ref, level):
    n = jnp.broadcast_to(shift_ref[pl.ds(level, 1), :], (T, shift_ref.shape[1]))
    return n == 0, n == 1, n == 2


def pick(load, start, shift_is):
    return jnp.where(
        shift_is[0], load(start), jnp.where(shift_is[1], load(start + 1), load(start + 2))
    )


def pick_back(load, start, shift_is):
    return jnp.where(
        shift_is[0], load(start), jnp.where(shift_is[1], load(start - 1), load(start - 2))
    )


def pick_first(load, shift_is):
    first = load(0)
    two_down = jnp.concatenate([first[T - 2 : T], first[0 : T - 2]], axis=0)
    one_down = jnp.concatenate([first[T - 1 : T], first[0 : T - 1]], axis=0)
    return jnp.where(shift_is[0], two_down, jnp.where(shift_is[1], one_down, first))


def pick_last(load, shift_is):
    first = load(0)
    two_up = jnp.concatenate([first[T - 2 : T], first[0 : T - 2]], axis=0)
    one_up = jnp.concatenate([first[T - 1 : T], first[0 : T - 1]], axis=0)
    return jnp.where(shift_is[0], two_up, one_up)


def fir(weights, load, start):
    total = weights[0] * load(start)
    for k in range(1, LEFT + RIGHT + 1):
        total = total + weights[k] * load(start + k)
    return total


def floor_parts(advected):
    square = advected * advected + FLOOR2
    root = lax.rsqrt(square)
    return square * root, advected * root


def pack_right_kernel(t_hbm, s_hbm, f_hbm, area_hbm, n_hbm, out_ref, t_buf, s_buf, f_buf, area_buf, n_buf, sems, small):
    count, columns, rows = t_hbm.shape
    levels = f_hbm.shape[0]
    bins = count // levels
    chunks = sems.shape[1]
    per = levels // chunks
    t_rows, s_rows = t_buf.shape[1], s_buf.shape[1]

    def copies(c):
        span = pl.ds(c * per * bins, per * bins)
        return (
            pltpu.make_async_copy(t_hbm.at[span, pl.ds(columns - t_rows, t_rows), :], t_buf.at[span], sems.at[0, c]),
            pltpu.make_async_copy(s_hbm.at[span, pl.ds(columns - s_rows, s_rows), :], s_buf.at[span], sems.at[1, c]),
        )

    others = [
        pltpu.make_async_copy(n_hbm, n_buf, small.at[0]),
        pltpu.make_async_copy(f_hbm.at[:, pl.ds(columns - T, T), :], f_buf, small.at[1]),
        pltpu.make_async_copy(area_hbm.at[pl.ds(columns - T, T), :], area_buf, small.at[2]),
    ]
    others[0].start()
    for c in range(chunks):
        for copy in copies(c):
            copy.start()
    for copy in others[1:]:
        copy.start()
    width = HALO + MAXOFF
    end = out_ref.shape[0]
    row = T + count * width
    last = row + LEFT * levels
    out_ref[0:T, :] = jnp.zeros((T, rows), jnp.float32)
    out_ref[last + MAXOFF : end, :] = jnp.zeros((end - last - MAXOFF, rows), jnp.float32)
    others[0].wait()

    def level_body(level, _):
        @pl.when(level % per == 0)
        def _():
            for copy in copies(level // per):
                copy.wait()

        unshifted = n_buf[pl.ds(level, 1), :] == 0

        def bin_body(b, _):
            lb = level * bins + b
            row = T + lb * width
            out_ref[pl.ds(row, HALO), :] = t_buf[lb, t_rows - HALO : t_rows, :]
            second = s_buf[lb, s_rows - 1 : s_rows, :]
            out_ref[pl.ds(row + HALO, 1), :] = jnp.where(unshifted, s_buf[lb, s_rows - 2 : s_rows - 1, :], second)
            out_ref[pl.ds(row + HALO + 1, 1), :] = second
            return 0

        lax.fori_loop(0, bins, bin_body, 0, unroll=15)
        return 0

    lax.fori_loop(0, levels, level_body, 0)
    for copy in others[1:]:
        copy.wait()
    for level in range(levels):
        out_ref[row + LEFT * level : row + LEFT * (level + 1), :] = f_buf[level, T - LEFT : T, :]
    out_ref[last : last + MAXOFF, :] = area_buf[T - MAXOFF : T, :]


def shifted_weights(f_of, area_of, cell, shift_is):
    face = pick(f_of, cell, shift_is)
    west = pick(f_of, cell - 1, shift_is)
    area = pick(area_of, cell, shift_is)
    return area, tap_weights(face, west, 1.0 / area, shift_is)


def each_chunk(level, per, act):
    @pl.when(level % per == 0)
    def _():
        act(level // per)


def interior_kernel(
    t_hbm, s_hbm, f_ref, area_ref, n_ref,
    t0_ref, s0_ref, t2_ref, s2_ref, ratio_ref, pos_ref, seed_ref, w_ref, ap_ref, red_ref, out_ref,
    t_buf, s_buf, part, in_sems,
):
    count, columns, rows = t_hbm.shape
    levels = f_ref.shape[0]
    bins = count // levels
    chunks = in_sems.shape[1]
    per = levels // chunks
    tiles = range(1, columns // T)
    last = columns - T
    width = 2 * HALO

    def copies_in(c):
        span = pl.ds(c * per * bins, per * bins)
        return (
            pltpu.make_async_copy(t_hbm.at[span], t_buf.at[span], in_sems.at[0, c]),
            pltpu.make_async_copy(s_hbm.at[span], s_buf.at[span], in_sems.at[1, c]),
        )

    for c in range(chunks):
        for copy in copies_in(c):
            copy.start()
    row = count * width
    for level in range(levels):
        out_ref[row + HALO * level : row + HALO * (level + 1), :] = f_ref[level, 0:HALO, :]
    row = row + HALO * levels
    out_ref[row : row + HALO, :] = area_ref[0:HALO, :]
    end = out_ref.shape[0]
    out_ref[row + HALO : end, :] = jnp.zeros((end - row - HALO, rows), jnp.float32)

    def level_body(level, _):
        def arrive(c):
            for copy in copies_in(c):
                copy.wait()

        each_chunk(level, per, arrive)
        shift_is = masks(n_ref, level)
        own = []
        for v in tiles:
            area, w = shifted_weights(
                lambda r: f_ref[level, pl.ds(r, T), :], lambda r: area_ref[pl.ds(r, T), :], T * v - OFF, shift_is
            )
            own.append((area, w))
            ap_ref[level, T * v : T * v + T, :] = area
            for k, value in enumerate(w):
                w_ref[level, k, T * v : T * v + T, :] = value
        for b in range(bins):
            lb = level * bins + b
            mass = None
            for v in range(columns // T):
                value = t_buf[lb, T * v : T * v + T, :]
                if v == 0:
                    t0_ref[lb, T : 2 * T, :] = value
                if v == columns // T - 1:
                    t2_ref[lb, 0:T, :] = value
                value = area_ref[T * v : T * v + T, :] * value
                mass = value if mass is None else mass + value
            early = pick_first(lambda r: s_buf[lb, pl.ds(r, T), :], shift_is)
            s0_ref[lb] = early
            s2_ref[lb] = pick_last(lambda r: s_buf[lb, pl.ds(last + r, T), :], shift_is)
            out_ref[pl.ds(lb * width, HALO), :] = t_buf[lb, 0:HALO, :]
            out_ref[pl.ds(lb * width + HALO, HALO), :] = early[0:HALO]
            after = dot = None
            for v, (area, w) in zip(tiles, own):
                cell = T * v - OFF
                advected = fir(w, lambda r: t_buf[lb, pl.ds(r, T), :], cell - LEFT)
                positive, ratio = floor_parts(advected)
                ratio_ref[lb, T * v : T * v + T, :] = ratio
                pos_ref[lb, T * v : T * v + T, :] = positive
                seed = pick(lambda r: s_buf[lb, pl.ds(r, T), :], cell, shift_is)
                seed_ref[lb, T * v : T * v + T, :] = seed
                after = area * positive if after is None else after + area * positive
                dot = seed * positive if dot is None else dot + seed * positive
            for k, value in enumerate((mass, after, dot)):
                part[k, pl.ds(lb * T, T), :] = value
        return 0

    lax.fori_loop(0, levels, level_body, 0)
    reduce_rows(part, red_ref, 3, count)


def reduce_rows(part, red_ref, kinds, count):
    def body(g, _):
        for k in range(kinds):
            total = part[k, pl.ds(g * T * T, T, stride=T), :]
            for s in range(1, T):
                total = total + part[k, pl.ds(g * T * T + s, T, stride=T), :]
            red_ref[k, pl.ds(g * T, T), :] = total
        return 0

    lax.fori_loop(0, count // T, body, 0, unroll=5)
    rest = red_ref.shape[1] - count
    for k in range(kinds):
        red_ref[k, pl.ds(count, rest), :] = jnp.zeros((rest, red_ref.shape[2]), jnp.float32)


def left_kernel(
    m_ref, t0_in, s0_ref, ratio_in, pos_in, seed_in, w_in, ap_in, red_ref, f_ref, area_ref, n_ref,
    t0_ref, ratio_ref, pos_ref, seed_ref, w_ref, ap_ref, sum_ref,
    part, red_new, f_buf, area_buf,
):
    count = t0_ref.shape[0]
    levels, _, rows = f_ref.shape
    bins = count // levels
    width = HALO + MAXOFF
    f_row = T + count * width
    area_row = f_row + LEFT * levels
    area_buf[0:T, :] = m_ref[area_row - (T - MAXOFF) : area_row + MAXOFF, :]
    area_buf[T : 2 * T, :] = area_ref[0:T, :]
    cell = T - OFF
    sublane = lax.broadcasted_iota(jnp.int32, (T, rows), 0)

    def level_body(level, _):
        shift_is = masks(n_ref, level)
        remote = sublane + jnp.broadcast_to(n_ref[pl.ds(level, 1), :], (T, rows)) < OFF
        f_buf[0:T, :] = m_ref[pl.ds(f_row + LEFT * level - (T - LEFT), T), :]
        f_buf[T : 2 * T, :] = f_ref[level, 0:T, :]
        area, w = shifted_weights(
            lambda r: f_buf[pl.ds(r, T), :], lambda r: area_buf[pl.ds(r, T), :], cell, shift_is
        )
        ap_ref[level, 0:T, :] = area
        for k, value in enumerate(w):
            w_ref[level, k, 0:T, :] = value
        for b in range(bins):
            lb = level * bins + b
            t0_ref[lb, 0:T, :] = m_ref[pl.ds(T + lb * width - (T - HALO), T), :]
        for b in range(bins):
            lb = level * bins + b
            advected = fir(w, lambda r: t0_ref[lb, pl.ds(r, T), :], cell - LEFT)
            positive, ratio = floor_parts(advected)
            ratio_ref[lb, 0:T, :] = ratio
            pos_ref[lb, 0:T, :] = positive
            seed = jnp.where(remote, m_ref[pl.ds(T + lb * width + HALO, T), :], s0_ref[lb])
            seed_ref[lb, 0:T, :] = seed
            part[0, pl.ds(lb * T, T), :] = area * positive
            part[1, pl.ds(lb * T, T), :] = seed * positive
        return 0

    lax.fori_loop(0, levels, level_body, 0)
    reduce_rows(part, red_new, 2, count)
    lines = []
    for k in range(3):
        for half in range(2):
            span = pl.ds(half * LANES, LANES)
            values = red_ref[k, span, :]
            if k:
                values = values + red_new[k - 1, span, :]
            lines.append(jnp.sum(values.T, axis=0, keepdims=True))
    lines.append(jnp.zeros((T - len(lines), rows), jnp.float32))
    sum_ref[...] = jnp.broadcast_to(jnp.concatenate(lines, axis=0)[None], sum_ref.shape)


def middle_kernel(
    ratio_ref, pos_in, seed_ref, w_ref, ap_ref, n_ref, sum_in,
    x_ref, y_ref, own_ref, pos_ref, sum_ref,
    x_buf, y_buf,
):
    levels = n_ref.shape[0]
    count = ratio_ref.shape[0]
    bins = count // levels
    tiles = ratio_ref.shape[1] // T
    taps = range(LEFT + RIGHT + 1)

    def level_body(level, _):
        shift_is = masks(n_ref, level)
        areas = [ap_ref[level, T * v : T * v + T, :] for v in range(tiles)]
        for b in range(bins):
            lb = level * bins + b
            for v in range(tiles):
                part = slice(T * v, T * v + T)
                ratio = ratio_ref[lb, part, :]
                x_buf[b, part, :] = seed_ref[lb, part, :] * ratio
                y_buf[b, part, :] = areas[v] * ratio
            x_ref[lb, T * (tiles - 1) : T * tiles, :] = x_buf[b, T * (tiles - 1) : T * tiles, :]
            y_ref[lb, T * (tiles - 1) : T * tiles, :] = y_buf[b, T * (tiles - 1) : T * tiles, :]
        for q in range(tiles - 1):
            weights = [w_ref[level, k, pl.ds(T * q + OFF + LEFT - k, T), :] for k in taps]
            part = slice(T * q, T * q + T)
            for b in range(bins):
                lb = level * bins + b
                for buf, out in ((x_buf, x_ref), (y_buf, y_ref)):
                    total = weights[0] * buf[b, pl.ds(T * q + OFF + LEFT, T), :]
                    for k in taps[1:]:
                        total = total + weights[k] * buf[b, pl.ds(T * q + OFF + LEFT - k, T), :]
                    out[lb, part, :] = total
                own_ref[lb, part, :] = pick_back(lambda r: pos_ref[lb, pl.ds(r, T), :], T * q + OFF, shift_is)
        return 0

    lax.fori_loop(0, levels, level_body, 0)


def final_kernel(
    g_ref, m_ref, t2_in, s2_ref, x_ref, y_ref, own_ref, pos_in, w_ref, f_ref, area_ref, n_ref,
    next_hbm, adj_hbm, t2_ref, pos_ref,
    scale_ref, w_buf, s_buf, next_buf, adj_buf, f_buf, area_buf, out_sems,
):
    count, columns, rows = next_buf.shape
    levels = f_ref.shape[0]
    bins = count // levels
    peers = g_ref.shape[0]
    tiles = columns // T
    last = columns - T
    chunks = out_sems.shape[1]
    per = levels // chunks
    taps = range(LEFT + RIGHT + 1)
    width = 2 * HALO

    def copies_out(c, rest):
        span = pl.ds(c * per * bins, per * bins)
        part = pl.ds(last, T) if rest else pl.ds(0, last)
        return (
            pltpu.make_async_copy(next_buf.at[span, part, :], next_hbm.at[span, part, :], out_sems.at[0 + 2 * rest, c]),
            pltpu.make_async_copy(adj_buf.at[span, part, :], adj_hbm.at[span, part, :], out_sems.at[1 + 2 * rest, c]),
        )

    def leave(rest):
        def act(c):
            for copy in copies_out(c - 1, rest):
                copy.start()

        return act

    total = g_ref[0]
    for peer in range(1, peers):
        total = total + g_ref[peer]
    mass_before, mass_after, seed_dot = total[0:2], total[2:4], total[4:6]
    direct = seed_dot / mass_after
    rescale = mass_before / mass_after
    for k, value in enumerate((rescale, rescale * direct, direct)):
        for half in range(2):
            column = jnp.broadcast_to(value[half : half + 1], (LANES, LANES)).T
            scale_ref[k, pl.ds(half * LANES, LANES), :] = column
    def main_body(level, _):
        for q in range(tiles - 1):
            part = slice(T * q, T * q + T)
            area_own = area_ref[part, :]
            for b in range(bins):
                lb = level * bins + b
                rescale = scale_ref[0, pl.ds(lb, 1), :]
                value = area_own * scale_ref[2, pl.ds(lb, 1), :] + rescale * x_ref[lb, part, :]
                adj_buf[lb, part, :] = value - scale_ref[1, pl.ds(lb, 1), :] * y_ref[lb, part, :]
                next_buf[lb, part, :] = own_ref[lb, part, :] * rescale
        each_chunk(level + 1, per, leave(0))
        return 0

    lax.fori_loop(0, levels, main_body, 0)
    f_row = count * width
    area_row = f_row + HALO * levels
    area_buf[0:T, :] = area_ref[last:columns, :]
    area_buf[T : 2 * T, :] = m_ref[area_row : area_row + T, :]
    sublane = lax.broadcasted_iota(jnp.int32, (T, rows), 0)

    def level_body(level, _):
        shift_is = masks(n_ref, level)
        near = sublane + jnp.broadcast_to(n_ref[pl.ds(level, 1), :], (T, rows)) < OFF
        f_buf[0:T, :] = f_ref[level, last:columns, :]
        f_buf[T : 2 * T, :] = m_ref[pl.ds(f_row + HALO * level, T), :]
        area, w = shifted_weights(
            lambda r: f_buf[pl.ds(r, T), :], lambda r: area_buf[pl.ds(r, T), :], T - OFF, shift_is
        )
        for k in taps:
            w_buf[k, 0:T, :] = w_ref[level, k, last:columns, :]
            w_buf[k, T : 2 * T, :] = w[k]
        weights = [w_buf[k, pl.ds(OFF + LEFT - k, T), :] for k in taps]
        for b in range(bins):
            lb = level * bins + b
            t2_ref[lb, T : 2 * T, :] = m_ref[pl.ds(lb * width, T), :]
        for b in range(bins):
            lb = level * bins + b
            rescale = scale_ref[0, pl.ds(lb, 1), :]
            feedback = scale_ref[1, pl.ds(lb, 1), :]
            advected = fir(w, lambda r: t2_ref[lb, pl.ds(r, T), :], T - OFF - LEFT)
            positive, ratio = floor_parts(advected)
            pos_ref[lb, columns : columns + T, :] = positive
            seed = jnp.where(near, s2_ref[lb], m_ref[pl.ds(lb * width + HALO, T), :])
            s_buf[b, 0:T, :] = rescale * x_ref[lb, last:columns, :] - feedback * y_ref[lb, last:columns, :]
            s_buf[b, T : 2 * T, :] = (rescale * seed - feedback * area) * ratio
        part = slice(last, columns)
        area_own = area_ref[part, :]
        for b in range(bins):
            lb = level * bins + b
            value = area_own * scale_ref[2, pl.ds(lb, 1), :]
            for k in taps:
                value = value + weights[k] * s_buf[b, pl.ds(OFF + LEFT - k, T), :]
            adj_buf[lb, part, :] = value
            own = pick_back(lambda r: pos_ref[lb, pl.ds(r, T), :], last + OFF, shift_is)
            next_buf[lb, part, :] = own * scale_ref[0, pl.ds(lb, 1), :]
        each_chunk(level + 1, per, leave(1))
        return 0

    lax.fori_loop(0, levels, level_body, 0)
    for c in range(chunks):
        for rest in range(2):
            for copy in copies_out(c, rest):
                copy.wait()


def padded(rows):
    return (rows + 2 * T - 1) // T * T


def shards(tracer, courant_frac, departure_shift, cell_area, adjoint_seed):
    levels, bins, columns, rows = tracer.shape
    count = levels * bins
    f32 = jnp.float32
    tile = lax.axis_size("tile")
    to_right = [(i, (i + 1) % tile) for i in range(tile)]
    to_left = [(target, source) for source, target in to_right]
    hbm = pl.BlockSpec(memory_space=pl.ANY)
    vmem = pl.BlockSpec(memory_space=pltpu.VMEM)
    params = pltpu.CompilerParams(vmem_limit_bytes=VMEM_LIMIT)
    dma = pltpu.SemaphoreType.DMA
    taps = LEFT + RIGHT + 1

    def held(x):
        return pltpu.with_memory_space_constraint(x, pltpu.VMEM)

    def far(x):
        return pltpu.with_memory_space_constraint(x, pltpu.HBM)

    def cost(flops, nbytes):
        return pl.CostEstimate(flops=flops, bytes_accessed=nbytes, transcendentals=0)

    size = 4 * count * columns * rows
    t = tracer.reshape(count, columns, rows)
    seed = adjoint_seed.reshape(count, columns, rows)

    message = pl.pallas_call(
        pack_right_kernel,
        out_shape=jax.ShapeDtypeStruct((padded(T + count * (HALO + MAXOFF) + LEFT * levels + MAXOFF), rows), f32),
        in_specs=[hbm] * 5,
        out_specs=vmem,
        scratch_shapes=[
            pltpu.VMEM((count, HALO, rows), f32),
            pltpu.VMEM((count, MAXOFF, rows), f32),
            pltpu.VMEM((levels, T, rows), f32),
            pltpu.VMEM((T, rows), f32),
            pltpu.VMEM((levels, rows), jnp.int32),
            dma((2, 2)),
            dma((3,)),
        ],
        compiler_params=params,
        cost_estimate=cost(0, size),
        name="pack_right",
    )(far(t), far(seed), far(courant_frac), far(cell_area), far(departure_shift))
    from_left = lax.ppermute(message, "tile", to_right)

    strip = pltpu.VMEM((count, T, rows), f32)
    two_strips = pltpu.VMEM((count, 2 * T, rows), f32)
    whole = pltpu.VMEM((count, columns, rows), f32)
    wide = pltpu.VMEM((count, columns + T, rows), f32)
    w_shape = pltpu.VMEM((levels, taps, columns, rows), f32)
    ap_shape = pltpu.VMEM((levels, columns, rows), f32)
    left_rows = padded(2 * count * HALO + HALO * levels + HALO)

    t0, s0, t2, s2, ratio, positive, seeds, w, ap, red, message_left = pl.pallas_call(
        interior_kernel,
        out_shape=(
            two_strips, strip, two_strips, strip, whole, wide, whole, w_shape, ap_shape,
            pltpu.VMEM((3, 2 * LANES, rows), f32),
            jax.ShapeDtypeStruct((left_rows, rows), f32),
        ),
        in_specs=[hbm, hbm, vmem, vmem, vmem],
        out_specs=(vmem,) * 11,
        scratch_shapes=[
            pltpu.VMEM((count, columns, rows), f32),
            pltpu.VMEM((count, columns, rows), f32),
            pltpu.VMEM((3, count * T, rows), f32),
            dma((2, CHUNKS)),
        ],
        compiler_params=params,
        cost_estimate=cost(30 * size, 4 * size),
        name="interior",
    )(far(t), far(seed), courant_frac, cell_area, departure_shift)

    from_left, message_left = lax.optimization_barrier((from_left, message_left))
    from_right = lax.ppermute(message_left, "tile", to_left)

    _, ratio, positive, seeds, w, ap, sums = pl.pallas_call(
        left_kernel,
        out_shape=(
            two_strips, whole, wide, whole, w_shape, ap_shape,
            pltpu.VMEM((tile, T, LANES), f32),
        ),
        in_specs=[vmem] * 12,
        out_specs=(vmem,) * 7,
        input_output_aliases={1: 0, 3: 1, 4: 2, 5: 3, 6: 4, 7: 5},
        scratch_shapes=[
            pltpu.VMEM((2, count * T, rows), f32),
            pltpu.VMEM((2, 2 * LANES, rows), f32),
            pltpu.VMEM((2 * T, rows), f32),
            pltpu.VMEM((2 * T, rows), f32),
        ],
        compiler_params=params,
        cost_estimate=cost(10 * size, size),
        name="left_edge",
    )(
        from_left, held(t0), held(s0), held(ratio), held(positive), held(seeds), held(w), held(ap), held(red),
        courant_frac, cell_area, departure_shift,
    )

    x, y, own, positive, sums = pl.pallas_call(
        middle_kernel,
        out_shape=(whole, whole, two_strips, wide, pltpu.VMEM((tile, T, LANES), f32)),
        in_specs=[vmem] * 7,
        out_specs=(vmem,) * 5,
        input_output_aliases={1: 3, 6: 4},
        scratch_shapes=[pltpu.VMEM((bins, columns, rows), f32), pltpu.VMEM((bins, columns, rows), f32)],
        compiler_params=params,
        cost_estimate=cost(30 * size, size),
        name="middle",
    )(held(ratio), held(positive), held(seeds), held(w), held(ap), departure_shift, held(sums))

    sums = lax.all_to_all(sums, "tile", 0, 0)

    tracer_next, tracer_adjoint, _, _ = pl.pallas_call(
        final_kernel,
        out_shape=(
            jax.ShapeDtypeStruct((count, columns, rows), f32),
            jax.ShapeDtypeStruct((count, columns, rows), f32),
            two_strips,
            wide,
        ),
        in_specs=[vmem] * 12,
        out_specs=(hbm, hbm, vmem, vmem),
        input_output_aliases={2: 2, 7: 3},
        scratch_shapes=[
            pltpu.VMEM((3, 2 * LANES, rows), f32),
            pltpu.VMEM((taps, 2 * T, rows), f32),
            pltpu.VMEM((bins, 2 * T, rows), f32),
            pltpu.VMEM((count, columns, rows), f32),
            pltpu.VMEM((count, columns, rows), f32),
            pltpu.VMEM((2 * T, rows), f32),
            pltpu.VMEM((2 * T, rows), f32),
            dma((4, CHUNKS)),
        ],
        compiler_params=params,
        cost_estimate=cost(10 * size, size),
        name="final",
    )(
        sums, from_right, held(t2), held(s2), held(x), held(y), held(own), held(positive), held(w),
        courant_frac, cell_area, departure_shift,
    )
    return tracer_next.reshape(tracer.shape), tracer_adjoint.reshape(tracer.shape)


def solution(mesh):
    return jax.shard_map(
        shards,
        mesh=mesh,
        in_specs=(
            P("group", None, "tile", None),
            P("group", "tile", None),
            P("group", None),
            P("tile", None),
            P("group", None, "tile", None),
        ),
        out_specs=(P("group", None, "tile", None), P("group", None, "tile", None)),
        check_vma=False,
    )
```

```python
import jax
import jax.numpy as jnp
from jax import lax
from jax.experimental import pallas as pl
from jax.experimental.pallas import tpu as pltpu
from jax.sharding import PartitionSpec as P

MAXOFF = 2
FLOOR2 = 0.1 * 0.1
LEFT, RIGHT = 3, 2
OFF = MAXOFF
HALO = LEFT + MAXOFF
T = 8
LANES = 128
VMEM_LIMIT = 20 * 2**20
CHUNKS = 4
HIGHEST = lax.Precision.HIGHEST


def tap_weights(face, west, inverse, shift_is):
    def taps(f):
        f2 = f * f
        f3 = f2 * f
        alpha = 3.0 * f2 - 2.0 * f3
        beta = f3 - f2
        gamma = f - 2.0 * f2 + f3
        return (
            beta * (-1.0 / 12.0),
            (7.0 / 12.0) * beta - (1.0 / 12.0) * gamma,
            alpha + (7.0 / 12.0) * (beta + gamma),
            (7.0 / 12.0) * gamma - (1.0 / 12.0) * beta,
            gamma * (-1.0 / 12.0),
        )

    east_taps, west_taps = taps(face), taps(west)
    weights = [west_taps[0] * inverse]
    for k in range(4):
        weights.append((west_taps[k + 1] - east_taps[k]) * inverse)
    weights.append(-east_taps[4] * inverse)
    is0, is1, is2 = shift_is
    rest = 1.0 - inverse
    weights[3] = weights[3] + jnp.where(is0, 1.0, inverse)
    weights[4] = weights[4] + jnp.where(is1, rest, 0.0)
    weights[5] = weights[5] + jnp.where(is2, rest, 0.0)
    return weights


def masks(shift_ref, level):
    n = jnp.broadcast_to(shift_ref[pl.ds(level, 1), :], (T, shift_ref.shape[1]))
    return n == 0, n == 1, n == 2


def pick(load, start, shift_is):
    return jnp.where(
        shift_is[0], load(start), jnp.where(shift_is[1], load(start + 1), load(start + 2))
    )


def pick_back(load, start, shift_is):
    return jnp.where(
        shift_is[0], load(start), jnp.where(shift_is[1], load(start - 1), load(start - 2))
    )


def pick_first(load, shift_is):
    first = load(0)
    two_down = jnp.concatenate([first[T - 2 : T], first[0 : T - 2]], axis=0)
    one_down = jnp.concatenate([first[T - 1 : T], first[0 : T - 1]], axis=0)
    return jnp.where(shift_is[0], two_down, jnp.where(shift_is[1], one_down, first))


def pick_last(load, shift_is):
    first = load(0)
    two_up = jnp.concatenate([first[T - 2 : T], first[0 : T - 2]], axis=0)
    one_up = jnp.concatenate([first[T - 1 : T], first[0 : T - 1]], axis=0)
    return jnp.where(shift_is[0], two_up, one_up)


def fir(weights, load, start):
    total = weights[0] * load(start)
    for k in range(1, LEFT + RIGHT + 1):
        total = total + weights[k] * load(start + k)
    return total


def floor_parts(advected):
    square = advected * advected + FLOOR2
    root = lax.rsqrt(square)
    return square * root, advected * root


def pack_right_kernel(t_hbm, s_hbm, f_hbm, area_hbm, n_hbm, out_ref, t_buf, s_buf, f_buf, area_buf, n_buf, sems, small):
    count, columns, rows = t_hbm.shape
    levels = f_hbm.shape[0]
    bins = count // levels
    chunks = sems.shape[1]
    per = levels // chunks
    t_rows, s_rows = t_buf.shape[1], s_buf.shape[1]

    def copies(c):
        span = pl.ds(c * per * bins, per * bins)
        return (
            pltpu.make_async_copy(t_hbm.at[span, pl.ds(columns - t_rows, t_rows), :], t_buf.at[span], sems.at[0, c]),
            pltpu.make_async_copy(s_hbm.at[span, pl.ds(columns - s_rows, s_rows), :], s_buf.at[span], sems.at[1, c]),
        )

    others = [
        pltpu.make_async_copy(n_hbm, n_buf, small.at[0]),
        pltpu.make_async_copy(f_hbm.at[:, pl.ds(columns - T, T), :], f_buf, small.at[1]),
        pltpu.make_async_copy(area_hbm.at[pl.ds(columns - T, T), :], area_buf, small.at[2]),
    ]
    others[0].start()
    for c in range(chunks):
        for copy in copies(c):
            copy.start()
    for copy in others[1:]:
        copy.start()
    width = HALO + MAXOFF
    end = out_ref.shape[0]
    row = T + count * width
    last = row + LEFT * levels
    out_ref[0:T, :] = jnp.zeros((T, rows), jnp.float32)
    out_ref[last + MAXOFF : end, :] = jnp.zeros((end - last - MAXOFF, rows), jnp.float32)
    others[0].wait()

    def level_body(level, _):
        @pl.when(level % per == 0)
        def _():
            for copy in copies(level // per):
                copy.wait()

        unshifted = n_buf[pl.ds(level, 1), :] == 0

        def bin_body(b, _):
            lb = level * bins + b
            row = T + lb * width
            out_ref[pl.ds(row, HALO), :] = t_buf[lb, t_rows - HALO : t_rows, :]
            second = s_buf[lb, s_rows - 1 : s_rows, :]
            out_ref[pl.ds(row + HALO, 1), :] = jnp.where(unshifted, s_buf[lb, s_rows - 2 : s_rows - 1, :], second)
            out_ref[pl.ds(row + HALO + 1, 1), :] = second
            return 0

        lax.fori_loop(0, bins, bin_body, 0, unroll=15)
        return 0

    lax.fori_loop(0, levels, level_body, 0)
    for copy in others[1:]:
        copy.wait()
    for level in range(levels):
        out_ref[row + LEFT * level : row + LEFT * (level + 1), :] = f_buf[level, T - LEFT : T, :]
    out_ref[last : last + MAXOFF, :] = area_buf[T - MAXOFF : T, :]


def shifted_weights(f_of, area_of, cell, shift_is):
    face = pick(f_of, cell, shift_is)
    west = pick(f_of, cell - 1, shift_is)
    area = pick(area_of, cell, shift_is)
    return area, tap_weights(face, west, 1.0 / area, shift_is)


def each_chunk(level, per, act):
    @pl.when(level % per == 0)
    def _():
        act(level // per)


def interior_kernel(
    t_hbm, s_hbm, f_ref, area_ref, n_ref,
    t0_ref, s0_ref, t2_ref, s2_ref, ratio_ref, pos_ref, seed_ref, w_ref, ap_ref, red_ref, out_ref,
    t_buf, s_buf, part, in_sems,
):
    count, columns, rows = t_hbm.shape
    levels = f_ref.shape[0]
    bins = count // levels
    chunks = in_sems.shape[1]
    per = levels // chunks
    tiles = range(1, columns // T)
    last = columns - T
    width = 2 * HALO

    def copies_in(c):
        span = pl.ds(c * per * bins, per * bins)
        return (
            pltpu.make_async_copy(t_hbm.at[span], t_buf.at[span], in_sems.at[0, c]),
            pltpu.make_async_copy(s_hbm.at[span], s_buf.at[span], in_sems.at[1, c]),
        )

    for c in range(chunks):
        for copy in copies_in(c):
            copy.start()
    row = count * width
    for level in range(levels):
        out_ref[row + HALO * level : row + HALO * (level + 1), :] = f_ref[level, 0:HALO, :]
    row = row + HALO * levels
    out_ref[row : row + HALO, :] = area_ref[0:HALO, :]
    end = out_ref.shape[0]
    out_ref[row + HALO : end, :] = jnp.zeros((end - row - HALO, rows), jnp.float32)

    def level_body(level, _):
        def arrive(c):
            for copy in copies_in(c):
                copy.wait()

        each_chunk(level, per, arrive)
        shift_is = masks(n_ref, level)
        own = []
        for v in tiles:
            area, w = shifted_weights(
                lambda r: f_ref[level, pl.ds(r, T), :], lambda r: area_ref[pl.ds(r, T), :], T * v - OFF, shift_is
            )
            own.append((area, w))
            ap_ref[level, T * v : T * v + T, :] = area
            for k, value in enumerate(w):
                w_ref[level, k, T * v : T * v + T, :] = value
        for b in range(bins):
            lb = level * bins + b
            mass = None
            for v in range(columns // T):
                value = t_buf[lb, T * v : T * v + T, :]
                if v == 0:
                    t0_ref[lb, T : 2 * T, :] = value
                if v == columns // T - 1:
                    t2_ref[lb, 0:T, :] = value
                value = area_ref[T * v : T * v + T, :] * value
                mass = value if mass is None else mass + value
            early = pick_first(lambda r: s_buf[lb, pl.ds(r, T), :], shift_is)
            s0_ref[lb] = early
            s2_ref[lb] = pick_last(lambda r: s_buf[lb, pl.ds(last + r, T), :], shift_is)
            out_ref[pl.ds(lb * width, HALO), :] = t_buf[lb, 0:HALO, :]
            out_ref[pl.ds(lb * width + HALO, HALO), :] = early[0:HALO]
            after = dot = None
            for v, (area, w) in zip(tiles, own):
                cell = T * v - OFF
                advected = fir(w, lambda r: t_buf[lb, pl.ds(r, T), :], cell - LEFT)
                positive, ratio = floor_parts(advected)
                ratio_ref[lb, T * v : T * v + T, :] = ratio
                pos_ref[lb, T * v : T * v + T, :] = positive
                seed = pick(lambda r: s_buf[lb, pl.ds(r, T), :], cell, shift_is)
                seed_ref[lb, T * v : T * v + T, :] = seed
                after = area * positive if after is None else after + area * positive
                dot = seed * positive if dot is None else dot + seed * positive
            for k, value in enumerate((mass, after, dot)):
                part[k, pl.ds(lb * T, T), :] = value
        return 0

    lax.fori_loop(0, levels, level_body, 0)
    reduce_rows(part, red_ref, 3, count)


def reduce_rows(part, red_ref, kinds, count):
    def body(g, _):
        for k in range(kinds):
            total = part[k, pl.ds(g * T * T, T, stride=T), :]
            for s in range(1, T):
                total = total + part[k, pl.ds(g * T * T + s, T, stride=T), :]
            red_ref[k, pl.ds(g * T, T), :] = total
        return 0

    lax.fori_loop(0, count // T, body, 0, unroll=5)
    rest = red_ref.shape[1] - count
    for k in range(kinds):
        red_ref[k, pl.ds(count, rest), :] = jnp.zeros((rest, red_ref.shape[2]), jnp.float32)


def left_kernel(
    m_ref, t0_in, s0_ref, ratio_in, pos_in, seed_in, w_in, ap_in, red_ref, f_ref, area_ref, n_ref,
    t0_ref, ratio_ref, pos_ref, seed_ref, w_ref, ap_ref, sum_ref,
    part, red_new, f_buf, area_buf,
):
    count = t0_ref.shape[0]
    levels, _, rows = f_ref.shape
    bins = count // levels
    width = HALO + MAXOFF
    f_row = T + count * width
    area_row = f_row + LEFT * levels
    area_buf[0:T, :] = m_ref[area_row - (T - MAXOFF) : area_row + MAXOFF, :]
    area_buf[T : 2 * T, :] = area_ref[0:T, :]
    cell = T - OFF
    sublane = lax.broadcasted_iota(jnp.int32, (T, rows), 0)

    def level_body(level, _):
        shift_is = masks(n_ref, level)
        remote = sublane + jnp.broadcast_to(n_ref[pl.ds(level, 1), :], (T, rows)) < OFF
        f_buf[0:T, :] = m_ref[pl.ds(f_row + LEFT * level - (T - LEFT), T), :]
        f_buf[T : 2 * T, :] = f_ref[level, 0:T, :]
        area, w = shifted_weights(
            lambda r: f_buf[pl.ds(r, T), :], lambda r: area_buf[pl.ds(r, T), :], cell, shift_is
        )
        ap_ref[level, 0:T, :] = area
        for k, value in enumerate(w):
            w_ref[level, k, 0:T, :] = value
        for b in range(bins):
            lb = level * bins + b
            t0_ref[lb, 0:T, :] = m_ref[pl.ds(T + lb * width - (T - HALO), T), :]
        for b in range(bins):
            lb = level * bins + b
            advected = fir(w, lambda r: t0_ref[lb, pl.ds(r, T), :], cell - LEFT)
            positive, ratio = floor_parts(advected)
            ratio_ref[lb, 0:T, :] = ratio
            pos_ref[lb, 0:T, :] = positive
            seed = jnp.where(remote, m_ref[pl.ds(T + lb * width + HALO, T), :], s0_ref[lb])
            seed_ref[lb, 0:T, :] = seed
            part[0, pl.ds(lb * T, T), :] = area * positive
            part[1, pl.ds(lb * T, T), :] = seed * positive
        return 0

    lax.fori_loop(0, levels, level_body, 0)
    reduce_rows(part, red_new, 2, count)
    lines = []
    for k in range(3):
        for half in range(2):
            span = pl.ds(half * LANES, LANES)
            values = red_ref[k, span, :]
            if k:
                values = values + red_new[k - 1, span, :]
            lines.append(jnp.sum(values.T, axis=0, keepdims=True))
    lines.append(jnp.zeros((T - len(lines), rows), jnp.float32))
    sum_ref[...] = jnp.broadcast_to(jnp.concatenate(lines, axis=0)[None], sum_ref.shape)


def middle_kernel(
    ratio_ref, pos_in, seed_ref, w_ref, ap_ref, n_ref, sum_in,
    x_ref, y_ref, own_ref, pos_ref, sum_ref,
    x_buf, y_buf,
):
    levels = n_ref.shape[0]
    count = ratio_ref.shape[0]
    bins = count // levels
    tiles = ratio_ref.shape[1] // T
    taps = range(LEFT + RIGHT + 1)

    def level_body(level, _):
        shift_is = masks(n_ref, level)
        areas = [ap_ref[level, T * v : T * v + T, :] for v in range(tiles)]
        for b in range(bins):
            lb = level * bins + b
            for v in range(tiles):
                part = slice(T * v, T * v + T)
                ratio = ratio_ref[lb, part, :]
                x_buf[b, part, :] = seed_ref[lb, part, :] * ratio
                y_buf[b, part, :] = areas[v] * ratio
            x_ref[lb, T * (tiles - 1) : T * tiles, :] = x_buf[b, T * (tiles - 1) : T * tiles, :]
            y_ref[lb, T * (tiles - 1) : T * tiles, :] = y_buf[b, T * (tiles - 1) : T * tiles, :]
        for q in range(tiles - 1):
            weights = [w_ref[level, k, pl.ds(T * q + OFF + LEFT - k, T), :] for k in taps]
            part = slice(T * q, T * q + T)
            for b in range(bins):
                lb = level * bins + b
                for buf, out in ((x_buf, x_ref), (y_buf, y_ref)):
                    total = weights[0] * buf[b, pl.ds(T * q + OFF + LEFT, T), :]
                    for k in taps[1:]:
                        total = total + weights[k] * buf[b, pl.ds(T * q + OFF + LEFT - k, T), :]
                    out[lb, part, :] = total
                own_ref[lb, part, :] = pick_back(lambda r: pos_ref[lb, pl.ds(r, T), :], T * q + OFF, shift_is)
        return 0

    lax.fori_loop(0, levels, level_body, 0)


def final_kernel(
    g_ref, m_ref, t2_in, s2_ref, x_ref, y_ref, own_ref, pos_in, w_ref, f_ref, area_ref, n_ref,
    next_hbm, adj_hbm, t2_ref, pos_ref,
    scale_ref, w_buf, s_buf, next_buf, adj_buf, f_buf, area_buf, out_sems,
):
    count, columns, rows = next_buf.shape
    levels = f_ref.shape[0]
    bins = count // levels
    peers = g_ref.shape[0]
    tiles = columns // T
    last = columns - T
    chunks = out_sems.shape[1]
    per = levels // chunks
    taps = range(LEFT + RIGHT + 1)
    width = 2 * HALO

    def copies_out(c, rest):
        span = pl.ds(c * per * bins, per * bins)
        part = pl.ds(last, T) if rest else pl.ds(0, last)
        return (
            pltpu.make_async_copy(next_buf.at[span, part, :], next_hbm.at[span, part, :], out_sems.at[0 + 2 * rest, c]),
            pltpu.make_async_copy(adj_buf.at[span, part, :], adj_hbm.at[span, part, :], out_sems.at[1 + 2 * rest, c]),
        )

    def leave(rest):
        def act(c):
            for copy in copies_out(c - 1, rest):
                copy.start()

        return act

    total = g_ref[0]
    for peer in range(1, peers):
        total = total + g_ref[peer]
    mass_before, mass_after, seed_dot = total[0:2], total[2:4], total[4:6]
    direct = seed_dot / mass_after
    rescale = mass_before / mass_after
    for k, value in enumerate((rescale, rescale * direct, direct)):
        for half in range(2):
            column = jnp.broadcast_to(value[half : half + 1], (LANES, LANES)).T
            scale_ref[k, pl.ds(half * LANES, LANES), :] = column
    def main_body(level, _):
        for q in range(tiles - 1):
            part = slice(T * q, T * q + T)
            area_own = area_ref[part, :]
            for b in range(bins):
                lb = level * bins + b
                rescale = scale_ref[0, pl.ds(lb, 1), :]
                value = area_own * scale_ref[2, pl.ds(lb, 1), :] + rescale * x_ref[lb, part, :]
                adj_buf[lb, part, :] = value - scale_ref[1, pl.ds(lb, 1), :] * y_ref[lb, part, :]
                next_buf[lb, part, :] = own_ref[lb, part, :] * rescale
        each_chunk(level + 1, per, leave(0))
        return 0

    lax.fori_loop(0, levels, main_body, 0, unroll=2)
    f_row = count * width
    area_row = f_row + HALO * levels
    area_buf[0:T, :] = area_ref[last:columns, :]
    area_buf[T : 2 * T, :] = m_ref[area_row : area_row + T, :]
    sublane = lax.broadcasted_iota(jnp.int32, (T, rows), 0)

    def level_body(level, _):
        shift_is = masks(n_ref, level)
        near = sublane + jnp.broadcast_to(n_ref[pl.ds(level, 1), :], (T, rows)) < OFF
        f_buf[0:T, :] = f_ref[level, last:columns, :]
        f_buf[T : 2 * T, :] = m_ref[pl.ds(f_row + HALO * level, T), :]
        area, w = shifted_weights(
            lambda r: f_buf[pl.ds(r, T), :], lambda r: area_buf[pl.ds(r, T), :], T - OFF, shift_is
        )
        for k in taps:
            w_buf[k, 0:T, :] = w_ref[level, k, last:columns, :]
            w_buf[k, T : 2 * T, :] = w[k]
        weights = [w_buf[k, pl.ds(OFF + LEFT - k, T), :] for k in taps]
        for b in range(bins):
            lb = level * bins + b
            t2_ref[lb, T : 2 * T, :] = m_ref[pl.ds(lb * width, T), :]
        for b in range(bins):
            lb = level * bins + b
            rescale = scale_ref[0, pl.ds(lb, 1), :]
            feedback = scale_ref[1, pl.ds(lb, 1), :]
            advected = fir(w, lambda r: t2_ref[lb, pl.ds(r, T), :], T - OFF - LEFT)
            positive, ratio = floor_parts(advected)
            pos_ref[lb, columns : columns + T, :] = positive
            seed = jnp.where(near, s2_ref[lb], m_ref[pl.ds(lb * width + HALO, T), :])
            s_buf[b, 0:T, :] = rescale * x_ref[lb, last:columns, :] - feedback * y_ref[lb, last:columns, :]
            s_buf[b, T : 2 * T, :] = (rescale * seed - feedback * area) * ratio
        part = slice(last, columns)
        area_own = area_ref[part, :]
        for b in range(bins):
            lb = level * bins + b
            value = area_own * scale_ref[2, pl.ds(lb, 1), :]
            for k in taps:
                value = value + weights[k] * s_buf[b, pl.ds(OFF + LEFT - k, T), :]
            adj_buf[lb, part, :] = value
            own = pick_back(lambda r: pos_ref[lb, pl.ds(r, T), :], last + OFF, shift_is)
            next_buf[lb, part, :] = own * scale_ref[0, pl.ds(lb, 1), :]
        each_chunk(level + 1, per, leave(1))
        return 0

    lax.fori_loop(0, levels, level_body, 0)
    for c in range(chunks):
        for rest in range(2):
            for copy in copies_out(c, rest):
                copy.wait()


def padded(rows):
    return (rows + 2 * T - 1) // T * T


def shards(tracer, courant_frac, departure_shift, cell_area, adjoint_seed):
    levels, bins, columns, rows = tracer.shape
    count = levels * bins
    f32 = jnp.float32
    tile = lax.axis_size("tile")
    to_right = [(i, (i + 1) % tile) for i in range(tile)]
    to_left = [(target, source) for source, target in to_right]
    hbm = pl.BlockSpec(memory_space=pl.ANY)
    vmem = pl.BlockSpec(memory_space=pltpu.VMEM)
    params = pltpu.CompilerParams(vmem_limit_bytes=VMEM_LIMIT)
    dma = pltpu.SemaphoreType.DMA
    taps = LEFT + RIGHT + 1

    def held(x):
        return pltpu.with_memory_space_constraint(x, pltpu.VMEM)

    def far(x):
        return pltpu.with_memory_space_constraint(x, pltpu.HBM)

    def cost(flops, nbytes):
        return pl.CostEstimate(flops=flops, bytes_accessed=nbytes, transcendentals=0)

    size = 4 * count * columns * rows
    t = tracer.reshape(count, columns, rows)
    seed = adjoint_seed.reshape(count, columns, rows)

    message = pl.pallas_call(
        pack_right_kernel,
        out_shape=jax.ShapeDtypeStruct((padded(T + count * (HALO + MAXOFF) + LEFT * levels + MAXOFF), rows), f32),
        in_specs=[hbm] * 5,
        out_specs=vmem,
        scratch_shapes=[
            pltpu.VMEM((count, HALO, rows), f32),
            pltpu.VMEM((count, MAXOFF, rows), f32),
            pltpu.VMEM((levels, T, rows), f32),
            pltpu.VMEM((T, rows), f32),
            pltpu.VMEM((levels, rows), jnp.int32),
            dma((2, 2)),
            dma((3,)),
        ],
        compiler_params=params,
        cost_estimate=cost(0, size),
        name="pack_right",
    )(far(t), far(seed), far(courant_frac), far(cell_area), far(departure_shift))
    from_left = lax.ppermute(message, "tile", to_right)

    strip = pltpu.VMEM((count, T, rows), f32)
    two_strips = pltpu.VMEM((count, 2 * T, rows), f32)
    whole = pltpu.VMEM((count, columns, rows), f32)
    wide = pltpu.VMEM((count, columns + T, rows), f32)
    w_shape = pltpu.VMEM((levels, taps, columns, rows), f32)
    ap_shape = pltpu.VMEM((levels, columns, rows), f32)
    left_rows = padded(2 * count * HALO + HALO * levels + HALO)

    t0, s0, t2, s2, ratio, positive, seeds, w, ap, red, message_left = pl.pallas_call(
        interior_kernel,
        out_shape=(
            two_strips, strip, two_strips, strip, whole, wide, whole, w_shape, ap_shape,
            pltpu.VMEM((3, 2 * LANES, rows), f32),
            jax.ShapeDtypeStruct((left_rows, rows), f32),
        ),
        in_specs=[hbm, hbm, vmem, vmem, vmem],
        out_specs=(vmem,) * 11,
        scratch_shapes=[
            pltpu.VMEM((count, columns, rows), f32),
            pltpu.VMEM((count, columns, rows), f32),
            pltpu.VMEM((3, count * T, rows), f32),
            dma((2, CHUNKS)),
        ],
        compiler_params=params,
        cost_estimate=cost(30 * size, 4 * size),
        name="interior",
    )(far(t), far(seed), courant_frac, cell_area, departure_shift)

    from_left, message_left = lax.optimization_barrier((from_left, message_left))
    from_right = lax.ppermute(message_left, "tile", to_left)

    _, ratio, positive, seeds, w, ap, sums = pl.pallas_call(
        left_kernel,
        out_shape=(
            two_strips, whole, wide, whole, w_shape, ap_shape,
            pltpu.VMEM((tile, T, LANES), f32),
        ),
        in_specs=[vmem] * 12,
        out_specs=(vmem,) * 7,
        input_output_aliases={1: 0, 3: 1, 4: 2, 5: 3, 6: 4, 7: 5},
        scratch_shapes=[
            pltpu.VMEM((2, count * T, rows), f32),
            pltpu.VMEM((2, 2 * LANES, rows), f32),
            pltpu.VMEM((2 * T, rows), f32),
            pltpu.VMEM((2 * T, rows), f32),
        ],
        compiler_params=params,
        cost_estimate=cost(10 * size, size),
        name="left_edge",
    )(
        from_left, held(t0), held(s0), held(ratio), held(positive), held(seeds), held(w), held(ap), held(red),
        courant_frac, cell_area, departure_shift,
    )

    x, y, own, positive, sums = pl.pallas_call(
        middle_kernel,
        out_shape=(whole, whole, two_strips, wide, pltpu.VMEM((tile, T, LANES), f32)),
        in_specs=[vmem] * 7,
        out_specs=(vmem,) * 5,
        input_output_aliases={1: 3, 6: 4},
        scratch_shapes=[pltpu.VMEM((bins, columns, rows), f32), pltpu.VMEM((bins, columns, rows), f32)],
        compiler_params=params,
        cost_estimate=cost(30 * size, size),
        name="middle",
    )(held(ratio), held(positive), held(seeds), held(w), held(ap), departure_shift, held(sums))

    sums = lax.all_to_all(sums, "tile", 0, 0)

    tracer_next, tracer_adjoint, _, _ = pl.pallas_call(
        final_kernel,
        out_shape=(
            jax.ShapeDtypeStruct((count, columns, rows), f32),
            jax.ShapeDtypeStruct((count, columns, rows), f32),
            two_strips,
            wide,
        ),
        in_specs=[vmem] * 12,
        out_specs=(hbm, hbm, vmem, vmem),
        input_output_aliases={2: 2, 7: 3},
        scratch_shapes=[
            pltpu.VMEM((3, 2 * LANES, rows), f32),
            pltpu.VMEM((taps, 2 * T, rows), f32),
            pltpu.VMEM((bins, 2 * T, rows), f32),
            pltpu.VMEM((count, columns, rows), f32),
            pltpu.VMEM((count, columns, rows), f32),
            pltpu.VMEM((2 * T, rows), f32),
            pltpu.VMEM((2 * T, rows), f32),
            dma((4, CHUNKS)),
        ],
        compiler_params=params,
        cost_estimate=cost(10 * size, size),
        name="final",
    )(
        sums, from_right, held(t2), held(s2), held(x), held(y), held(own), held(positive), held(w),
        courant_frac, cell_area, departure_shift,
    )
    return tracer_next.reshape(tracer.shape), tracer_adjoint.reshape(tracer.shape)


def solution(mesh):
    return jax.shard_map(
        shards,
        mesh=mesh,
        in_specs=(
            P("group", None, "tile", None),
            P("group", "tile", None),
            P("group", None),
            P("tile", None),
            P("group", None, "tile", None),
        ),
        out_specs=(P("group", None, "tile", None), P("group", None, "tile", None)),
        check_vma=False,
    )
```
